256 devices in a mesh: chan: 8 (over z_hi, x), seq: 32 (over z_lo, y, core).
Axes of the slice: x: 4, y: 4, z: 8 (z_hi: 2, z_lo: 4; z = z_hi * 4 + z_lo), core: 2. Of those that a mesh axis runs over, the one named last changes fastest.
Arguments:
- query_input: bfloat16 [16384, 4096], P('seq', 'chan'), may hold values from -6 to 6
- key_input: bfloat16 [16384, 4096], P('seq', 'chan'), may hold values from -6 to 6
- value_input: bfloat16 [16384, 4096], P('seq', 'chan'), may hold values from -6 to 6
- filter_taps: bfloat16 [16384, 4096], P('seq', 'chan'), may hold values from -2 to 2
- short_taps: float32 [3, 3, 4096], P(None, None, 'chan'), may hold values from -3 to 3
- skip_gain: float32 [4096], P('chan'), may hold values from -3 to 3
Outputs:
- operator_out: bfloat16 [16384, 4096], P('seq', 'chan')
The draws below stay inside these ranges and needn't reach their ends.
All inputs are finite; a program needn't handle non-finite values.
Results may differ from the reference program's by a relative error of at most 0.001.
Values may be sent and summed in bfloat16 or wider, within the bound.
No kernel may reach another device: no remote copies, remote signals or barrier semaphores. Data moves between devices by JAX's collectives and lax.ppermute only.
A program may use at most 128 MiB of HBM per device.

```python
import math
import jax
import jax.numpy as jnp
from jax import lax

D = 4096
TAPS = 3
TOKENS = 16384


def draw_filter_taps(key, part):
    key = jax.random.fold_in(key, 7)
    key_noise, key_coin, key_rate, key_cut, key_tail, key_slow = jax.random.split(key, 6)
    noise = jax.random.normal(key_noise, (TOKENS, D), jnp.float32)
    tail_noise = jax.random.normal(key_tail, (TOKENS, D), jnp.float32)
    slow_percent = 60
    slow_flag = jax.random.randint(key_coin, (D,), 0, 100) < slow_percent
    spread = jax.random.uniform(key_rate, (D,), jnp.float32)
    slow_rate = 0.1 / TOKENS * jnp.exp(spread * math.log(20.0))
    fast_rate = 2.0 / TOKENS * jnp.exp(spread * math.log(0.015 * TOKENS))
    decay_rate = jnp.where(slow_flag, slow_rate, fast_rate)
    tail_spread = jax.random.uniform(key_slow, (D,), jnp.float32)
    tail_rate = 0.05 / TOKENS * jnp.exp(tail_spread * math.log(10.0))
    lag_index = jnp.arange(TOKENS, dtype=jnp.int32)[:, None]
    lag_float = lag_index.astype(jnp.float32)
    cut_points = jax.random.randint(key_cut, (3,), 1, TOKENS)
    drops = jnp.sum((lag_index >= cut_points[None, :]).astype(jnp.float32), axis=1, keepdims=True)
    envelope = jnp.exp(-decay_rate[None, :] * lag_float) * jnp.sqrt(2.0 * decay_rate)[None, :]
    tail_envelope = 0.25 / math.sqrt(TOKENS) * jnp.exp(-tail_rate[None, :] * lag_float)
    taps = (noise * envelope + tail_noise * tail_envelope) * jnp.power(0.6, drops)
    return taps.astype(jnp.bfloat16)


def levels(key, shape, cuts, smallest, largest):
    gain, own = 1.0, jax.random.fold_in(key, 6)
    for position, parts in cuts:
        steps = jnp.exp(jax.random.uniform(jax.random.fold_in(own, position), (parts,), jnp.float32, smallest / len(cuts), largest / len(cuts)))
        gain = gain * jnp.repeat(steps, shape[position] // parts).reshape([-1 if axis == position else 1 for axis in range(len(shape))])
    return gain


def gaussian(rng, dims, scale, limit, cuts=(), kind=jnp.bfloat16):
    drawn = scale * jax.random.normal(rng, dims, jnp.float32)
    if cuts:
        drawn = drawn * levels(rng, dims, cuts, -0.22, 0.18)
    return jnp.clip(drawn, -limit, limit).astype(kind)


def setup_inputs(seed: int = 0) -> dict:
    seeds = jax.random.split(jax.random.key(seed), 7)
    return {
        "query_input": gaussian(seeds[0], (TOKENS, D), 1.0, 6.0, ((0, 32), (1, 8))),
        "key_input": gaussian(seeds[1], (TOKENS, D), 1.0, 6.0, ((0, 32), (1, 8))),
        "value_input": gaussian(seeds[2], (TOKENS, D), 1.0, 6.0, ((0, 32), (1, 8))),
        "filter_taps": draw_filter_taps(jax.random.fold_in(seeds[6], 71), 0),
        "short_taps": gaussian(seeds[4], (3, TAPS, D), 0.6, 3.0, ((2, 8),), jnp.float32),
        "skip_gain": gaussian(seeds[5], (D,), 0.5, 3.0, ((0, 8),), jnp.float32),
    }


def causal_taps(rows, tap_weights):
    row_count = rows.shape[0]
    padded = jnp.pad(rows, ((2, 0), (0, 0)))
    return tap_weights[0] * padded[2:] + tap_weights[1] * padded[1:row_count + 1] + tap_weights[2] * padded[:row_count]


def reference(query_input, key_input, value_input, filter_taps, short_taps, skip_gain):
    query_mix = causal_taps(query_input.astype(jnp.float32), short_taps[0])
    key_mix = causal_taps(key_input.astype(jnp.float32), short_taps[1])
    value_mix = causal_taps(value_input.astype(jnp.float32), short_taps[2])
    product = key_mix * value_mix
    length = 2 * TOKENS
    group_size = 128
    data_blocks = product.T.reshape(D // group_size, group_size, TOKENS)
    filt_blocks = filter_taps.astype(jnp.float32).T.reshape(D // group_size, group_size, TOKENS)

    def convolve(block_pair):
        spectrum = jnp.fft.rfft(block_pair[0], n=length, axis=-1) * jnp.fft.rfft(block_pair[1], n=length, axis=-1)
        return jnp.fft.irfft(spectrum, n=length, axis=-1)[:, :TOKENS]

    convolved = lax.map(convolve, (data_blocks, filt_blocks)).reshape(D, TOKENS).T
    return (query_mix * (convolved + skip_gain * product)).astype(jnp.bfloat16)
```

```python
import functools
import math

import jax
import jax.numpy as jnp
import ml_dtypes
import numpy as np
from jax import lax
from jax.experimental import pallas as pl
from jax.experimental.pallas import tpu as pltpu
from jax.sharding import PartitionSpec as P

F32 = jnp.float32
BF16 = jnp.bfloat16

SIDE = 128
LENGTH = SIDE * SIDE
PACK = 16
BLOCKS = 32
TOKENS = 512
CHANS = 512
QUARTERS = TOKENS // SIDE
GROUP = 128
SENDS = GROUP // PACK
IN_TILES = 2 * QUARTERS + 1
OUT_TILES = QUARTERS + 1

SPAN = 252.0
DROP = 125.5
TINY = 1e-35


def split_const(table):
    hi = table.astype(ml_dtypes.bfloat16)
    lo = (table - hi.astype(np.float64)).astype(ml_dtypes.bfloat16)
    return hi, lo


def tables():
    n = np.arange(SIDE, dtype=np.float64)
    ang = 2.0 * np.pi / SIDE * np.outer(n - 0.25, n)
    first = np.concatenate([np.cos(ang), -np.sin(ang)], 0)
    last = np.concatenate([np.cos(ang).T, -np.sin(ang).T], 1) / LENGTH
    tw = 2.0 * np.pi / LENGTH * np.outer(n - 0.25, n)
    mid = 2.0 * np.pi / SIDE * (np.outer(n, n) % SIDE)
    cos, sin = np.cos(mid), np.sin(mid)
    fwd = np.block([[cos, -sin], [sin, cos]])
    inv = np.block([[cos, sin], [-sin, cos]])
    first_hi, first_lo = split_const(first)
    last_hi, last_lo = split_const(last)
    fwd_hi, fwd_lo = split_const(fwd)
    inv_hi, inv_lo = split_const(inv)
    return (
        np.concatenate([first_hi, first_hi, first_lo], 1),
        np.concatenate([first_hi, first_lo], 1),
        np.concatenate([fwd_hi, fwd_hi, fwd_lo], 0),
        np.concatenate([inv_hi, inv_hi, inv_lo], 0),
        np.concatenate([last_hi, last_hi, last_lo], 1),
        np.cos(tw).astype(np.float32),
        np.sin(tw).astype(np.float32),
    )


def split(x):
    hi = x.astype(BF16)
    lo = (x - hi.astype(F32)).astype(BF16)
    return hi, lo


def scale_up(largest):
    return jnp.maximum(largest * 1.004, TINY).astype(BF16).astype(F32)


def encode(x, inverse_scale):
    y = jnp.exp2(SPAN * jnp.sqrt(jnp.abs(x) * inverse_scale) - DROP)
    return jnp.where(x < 0.0, -y, y)


def decode(y, scale):
    g = (jnp.log2(jnp.abs(y)) + DROP) * (1.0 / SPAN)
    x = g * g * scale
    return jnp.where(y < 0.0, -x, x)


def mixed(rows, before, taps, pad_ref):
    count = rows.shape[0]
    pad_ref[pl.ds(8, count), :] = rows
    pad_ref[6:8, :] = before
    return (
        taps[0:1] * rows
        + taps[1:2] * pad_ref[pl.ds(7, count), :]
        + taps[2:3] * pad_ref[pl.ds(6, count), :]
    )


def front_kernel(key_ref, value_ref, filter_ref, taps_ref, out_ref, pad_ref, edge_ref):
    zero = jnp.zeros((2, GROUP), F32)
    key = key_ref[...].astype(F32)
    value = value_ref[...].astype(F32)
    product = mixed(key, zero, taps_ref[1], pad_ref) * mixed(value, zero, taps_ref[2], pad_ref)
    scale = scale_up(jnp.max(jnp.abs(product), axis=0, keepdims=True))
    code = encode(product, 1.0 / scale)

    edge_ref[...] = jnp.zeros_like(edge_ref)
    edge_ref[0:1, :] = scale
    for place, (rows, taps) in enumerate(((key, taps_ref[1]), (value, taps_ref[2]))):
        first, second = rows[0:1], rows[1:2]
        before, last = rows[TOKENS - 2 : TOKENS - 1], rows[TOKENS - 1 :]
        parts = (
            taps[0:1] * first,
            taps[0:1] * second + taps[1:2] * first,
            taps[1:2] * last + taps[2:3] * before,
            taps[2:3] * last,
        )
        for i, part in enumerate(parts):
            hi, lo = split(part)
            row = 8 + place * 8 + 2 * i
            edge_ref[row : row + 1, :] = hi.astype(F32)
            edge_ref[row + 1 : row + 2, :] = lo.astype(F32)

    def put(tile, block):
        out_ref[:, tile * PACK : (tile + 1) * PACK, :] = block.T.astype(BF16).reshape(SENDS, PACK, SIDE)

    for q in range(QUARTERS):
        rows = slice(q * SIDE, (q + 1) * SIDE)
        put(q, code[rows])
        put(QUARTERS + q, filter_ref[rows, :].astype(F32))
    put(2 * QUARTERS, edge_ref[...])


def middle_kernel(in_ref, first_ref, first_exact_ref, fwd_ref, inv_ref, last_ref, cos_ref, sin_ref, out_ref, prod_ref, filt_ref, conv_ref):
    rows = BLOCKS * QUARTERS * PACK
    edge = in_ref[:, 2 * QUARTERS * PACK :, :].astype(F32)
    scale = edge[:, :, 0:1]
    for q in range(QUARTERS):
        prod_ref[:, q] = decode(in_ref[:, q * PACK : (q + 1) * PACK, :].astype(F32), scale)
        filt_ref[:, q] = in_ref[:, (QUARTERS + q) * PACK : (QUARTERS + q + 1) * PACK, :].astype(F32)

    def part(place, i):
        lane = 8 + place * 8 + 2 * i
        return edge[:, :, lane : lane + 1] + edge[:, :, lane + 1 : lane + 2]

    def behind(x):
        return jnp.concatenate([jnp.zeros_like(x[:1]), x[:-1]], 0)

    first = (part(0, 0) + behind(part(0, 2))) * (part(1, 0) + behind(part(1, 2)))
    second = (part(0, 1) + behind(part(0, 3))) * (part(1, 1) + behind(part(1, 3)))
    lane = lax.broadcasted_iota(jnp.int32, (BLOCKS, PACK, SIDE), 2)
    prod_ref[:, 0] = jnp.where(lane == 0, first, jnp.where(lane == 1, second, prod_ref[:, 0]))

    prod_rows = prod_ref.reshape(rows, SIDE)
    filt_rows = filt_ref.reshape(rows, SIDE)
    conv_rows = conv_ref.reshape(rows, SIDE)

    def halves(x):
        return x[:SIDE], x[SIDE:]

    def one_pair(pair, carry):
        chans = [2 * pair, 2 * pair + 1]
        cos, sin = cos_ref[...], sin_ref[...]

        def channels(ref):
            return jnp.concatenate([ref[pl.ds(c, SIDE, stride=PACK), :] for c in chans], 1)

        hi, lo = split(channels(prod_rows))
        data = jnp.dot(first_ref[...], jnp.concatenate([hi, lo, hi], 0), preferred_element_type=F32)
        taps = channels(filt_rows).astype(BF16)
        filt = jnp.dot(first_exact_ref[...], jnp.concatenate([taps, taps], 0), preferred_element_type=F32)

        lhs = []
        for block in (data, filt):
            for i in range(2):
                re, im = halves(block[:, i * SIDE : (i + 1) * SIDE])
                both = jnp.concatenate([re * cos + im * sin, im * cos - re * sin], 1)
                hi, lo = split(both)
                lhs.append(jnp.concatenate([hi, lo, hi], 1))
        spectra = jnp.dot(jnp.concatenate(lhs, 0), fwd_ref[...], preferred_element_type=F32)
        x, h = spectra[: 2 * SIDE], spectra[2 * SIDE :]
        x_re, x_im, h_re, h_im = x[:, :SIDE], x[:, SIDE:], h[:, :SIDE], h[:, SIDE:]
        z = jnp.concatenate([x_re * h_re - x_im * h_im, x_re * h_im + x_im * h_re], 1)
        hi, lo = split(z)
        back = jnp.dot(jnp.concatenate([hi, lo, hi], 1), inv_ref[...], preferred_element_type=F32)
        cols = []
        for i in range(2):
            re, im = back[i * SIDE : (i + 1) * SIDE, :SIDE], back[i * SIDE : (i + 1) * SIDE, SIDE:]
            cols.append(jnp.concatenate([re * cos - im * sin, im * cos + re * sin], 0))
        hi, lo = split(jnp.concatenate(cols, 1))
        y = jnp.dot(last_ref[...], jnp.concatenate([hi, lo, hi], 0), preferred_element_type=F32)
        for i, c in enumerate(chans):
            conv_rows[pl.ds(c, SIDE, stride=PACK), :] = y[:, i * SIDE : (i + 1) * SIDE]
        return carry

    lax.fori_loop(0, PACK // 2, one_pair, 0)

    conv = [conv_ref[:, q] for q in range(QUARTERS)]
    largest = functools.reduce(jnp.maximum, [jnp.abs(c) for c in conv])
    scale = scale_up(jnp.max(largest, axis=2, keepdims=True))
    inverse = 1.0 / scale
    for q in range(QUARTERS):
        out_ref[:, q * PACK : (q + 1) * PACK, :] = encode(conv[q], inverse).astype(BF16)
    out_ref[:, QUARTERS * PACK :, :] = jnp.broadcast_to(scale, (BLOCKS, PACK, SIDE)).astype(BF16)


def end_kernel(query_ref, key_ref, value_ref, halo_ref, taps_ref, gain_ref, conv_ref, out_ref, pad_ref):
    def stream(place, ref):
        return mixed(ref[...].astype(F32), halo_ref[place].astype(F32), taps_ref[place], pad_ref)

    product = stream(1, key_ref) * stream(2, value_ref)
    query = stream(0, query_ref)
    direct = gain_ref[...] * product
    scale = conv_ref[:, QUARTERS * PACK :, 0:1].astype(F32)
    for q in range(QUARTERS):
        conv = decode(conv_ref[:, q * PACK : (q + 1) * PACK, :].astype(F32), scale)
        rows = slice(q * SIDE, (q + 1) * SIDE)
        out_ref[rows, :] = (query[rows] * (conv.reshape(GROUP, SIDE).T + direct[rows])).astype(BF16)


def local(consts, query_input, key_input, value_input, filter_taps, short_taps, skip_gain):
    steps = CHANS // GROUP
    rows_spec = pl.BlockSpec((TOKENS, GROUP), lambda i: (0, i))
    taps_spec = pl.BlockSpec((3, 3, GROUP), lambda i: (0, 0, i))
    params = pltpu.CompilerParams(vmem_limit_bytes=48 * 1024 * 1024)

    last_rows = jnp.stack([query_input[-2:], key_input[-2:], value_input[-2:]])
    pairs = [(i, i + 1) for i in range(BLOCKS - 1)]
    halo = lax.ppermute(last_rows, "seq", pairs)

    sent = pl.pallas_call(
        front_kernel,
        grid=(steps,),
        in_specs=[rows_spec, rows_spec, rows_spec, taps_spec],
        out_specs=pl.BlockSpec((SENDS, IN_TILES * PACK, SIDE), lambda i: (i, 0, 0)),
        out_shape=jax.ShapeDtypeStruct((BLOCKS, IN_TILES * PACK, SIDE), BF16),
        scratch_shapes=[pltpu.VMEM((TOKENS + 8, GROUP), F32), pltpu.VMEM((SIDE, GROUP), F32)],
        compiler_params=params,
        name="front",
    )(key_input, value_input, filter_taps, short_taps)
    arrived = lax.all_to_all(sent, "seq", split_axis=0, concat_axis=0, tiled=True)

    work = pltpu.VMEM((BLOCKS, QUARTERS, PACK, SIDE), F32)
    conv = pl.pallas_call(
        middle_kernel,
        out_shape=jax.ShapeDtypeStruct((BLOCKS, OUT_TILES * PACK, SIDE), BF16),
        scratch_shapes=[work, work, work],
        compiler_params=params,
        name="middle",
    )(arrived, *[jnp.asarray(c) for c in consts])
    returned = lax.all_to_all(conv, "seq", split_axis=0, concat_axis=0, tiled=True)

    return pl.pallas_call(
        end_kernel,
        grid=(steps,),
        in_specs=[
            rows_spec,
            rows_spec,
            rows_spec,
            pl.BlockSpec((3, 2, GROUP), lambda i: (0, 0, i)),
            taps_spec,
            pl.BlockSpec((1, GROUP), lambda i: (0, i)),
            pl.BlockSpec((SENDS, OUT_TILES * PACK, SIDE), lambda i: (i, 0, 0)),
        ],
        out_specs=rows_spec,
        out_shape=jax.ShapeDtypeStruct((TOKENS, CHANS), BF16),
        scratch_shapes=[pltpu.VMEM((TOKENS + 8, GROUP), F32)],
        compiler_params=params,
        name="end",
    )(query_input, key_input, value_input, halo, short_taps, skip_gain[None, :], returned)


def solution(mesh):
    placed = (
        P("seq", "chan"),
        P("seq", "chan"),
        P("seq", "chan"),
        P("seq", "chan"),
        P(None, None, "chan"),
        P("chan"),
    )
    return jax.shard_map(
        functools.partial(local, tables()),
        mesh=mesh,
        in_specs=placed,
        out_specs=P("seq", "chan"),
        check_vma=False,
    )
```

```python
import functools
import math

import jax
import jax.numpy as jnp
import ml_dtypes
import numpy as np
from jax import lax
from jax.experimental import pallas as pl
from jax.experimental.pallas import tpu as pltpu
from jax.sharding import PartitionSpec as P

F32 = jnp.float32
BF16 = jnp.bfloat16

SIDE = 128
LENGTH = SIDE * SIDE
PACK = 16
BLOCKS = 32
NEAR = 4
TOKENS = 512
CHANS = 512
QUARTERS = TOKENS // SIDE
BATCH = 8
UNROLL = 2
GROUP = 128
SENDS = GROUP // PACK
OUT_TILES = QUARTERS + 1

SPAN = 252.0
DROP = 125.5
TINY = 1e-35


def split_const(table):
    hi = table.astype(ml_dtypes.bfloat16)
    lo = (table - hi.astype(np.float64)).astype(ml_dtypes.bfloat16)
    return hi, lo


def tables():
    n = np.arange(SIDE, dtype=np.float64)
    ang = 2.0 * np.pi / SIDE * np.outer(n - 0.25, n)
    first = np.concatenate([np.cos(ang), -np.sin(ang)], 0)
    last = np.concatenate([np.cos(ang).T, -np.sin(ang).T], 1) / LENGTH
    tw = 2.0 * np.pi / LENGTH * np.outer(n - 0.25, n)
    mid = 2.0 * np.pi / SIDE * (np.outer(n, n) % SIDE)
    cos, sin = np.cos(mid), np.sin(mid)
    fwd = np.block([[cos, -sin], [sin, cos]])
    inv = np.block([[cos, sin], [-sin, cos]])
    first_hi, first_lo = split_const(first)
    last_hi, last_lo = split_const(last)
    fwd_hi, fwd_lo = split_const(fwd)
    inv_hi, inv_lo = split_const(inv)
    return (
        np.concatenate([first_hi, first_hi, first_lo], 1),
        np.concatenate([first_hi, first_lo], 1),
        np.concatenate([fwd_hi, fwd_hi, fwd_lo], 0),
        np.concatenate([inv_hi, inv_hi, inv_lo], 0),
        np.concatenate([last_hi, last_hi, last_lo], 1),
        np.cos(tw).astype(np.float32),
        np.sin(tw).astype(np.float32),
    )


def split(x):
    hi = x.astype(BF16)
    lo = (x - hi.astype(F32)).astype(BF16)
    return hi, lo


def scale_up(largest):
    return jnp.maximum(largest * 1.004, TINY).astype(BF16).astype(F32)


def encode(x, inverse_scale):
    y = jnp.exp2(SPAN * jnp.sqrt(jnp.abs(x) * inverse_scale) - DROP)
    return jnp.where(x < 0.0, -y, y)


def decode(y, scale):
    g = (jnp.log2(jnp.abs(y)) + DROP) * (1.0 / SPAN)
    x = g * g * scale
    return jnp.where(y < 0.0, -x, x)


def mixed(rows, before, taps, pad_ref):
    count = rows.shape[0]
    pad_ref[pl.ds(8, count), :] = rows
    pad_ref[6:8, :] = before
    return (
        taps[0:1] * rows
        + taps[1:2] * pad_ref[pl.ds(7, count), :]
        + taps[2:3] * pad_ref[pl.ds(6, count), :]
    )


def put(out_ref, tile, block):
    out_ref[:, tile * PACK : (tile + 1) * PACK, :] = block.T.astype(BF16).reshape(SENDS, PACK, SIDE)


def turn_kernel(*refs):
    *blocks, out_ref = refs
    for i, ref in enumerate(blocks):
        for q in range(QUARTERS):
            block = ref[q * SIDE : (q + 1) * SIDE, :].astype(F32).T.astype(BF16)
            out_ref[:, i, :, q * PACK : (q + 1) * PACK, :] = block.reshape(NEAR, 2, PACK, SIDE)


def product_kernel(key_ref, value_ref, taps_ref, out_ref, pad_ref, edge_ref):
    zero = jnp.zeros((2, GROUP), F32)
    key = key_ref[...].astype(F32)
    value = value_ref[...].astype(F32)
    product = mixed(key, zero, taps_ref[1], pad_ref) * mixed(value, zero, taps_ref[2], pad_ref)
    scale = scale_up(jnp.max(jnp.abs(product), axis=0, keepdims=True))
    code = encode(product, 1.0 / scale)

    edge_ref[...] = jnp.zeros_like(edge_ref)
    edge_ref[0:1, :] = scale
    for place, (rows, taps) in enumerate(((key, taps_ref[1]), (value, taps_ref[2]))):
        first, second = rows[0:1], rows[1:2]
        before, last = rows[TOKENS - 2 : TOKENS - 1], rows[TOKENS - 1 :]
        parts = (
            taps[0:1] * first,
            taps[0:1] * second + taps[1:2] * first,
            taps[1:2] * last + taps[2:3] * before,
            taps[2:3] * last,
        )
        for i, part in enumerate(parts):
            hi, lo = split(part)
            row = 8 + place * 8 + 2 * i
            edge_ref[row : row + 1, :] = hi.astype(F32)
            edge_ref[row + 1 : row + 2, :] = lo.astype(F32)

    for q in range(QUARTERS):
        put(out_ref, q, code[q * SIDE : (q + 1) * SIDE])
    put(out_ref, QUARTERS, edge_ref[...])


def rotated(block, cos, sin):
    lhs = []
    for i in range(block.shape[1] // SIDE):
        re, im = block[:SIDE, i * SIDE : (i + 1) * SIDE], block[SIDE:, i * SIDE : (i + 1) * SIDE]
        hi, lo = split(jnp.concatenate([re * cos + im * sin, im * cos - re * sin], 1))
        lhs.append(jnp.concatenate([hi, lo, hi], 1))
    return jnp.concatenate(lhs, 0)


def channels(rows, batch):
    return jnp.concatenate([rows[pl.ds(BATCH * batch + i, SIDE, stride=PACK), :] for i in range(BATCH)], 1)


def spectrum_kernel(place_ref, b0_ref, b1_ref, b2_ref, b3_ref, other_ref, first_ref, fwd_ref, cos_ref, sin_ref, out_ref, filt_ref):
    me = place_ref[0]
    z, y, core = me // 8, (me // 2) % 4, me % 2
    for dy, ref in enumerate((b0_ref, b1_ref, b2_ref, b3_ref)):
        for dz in range(NEAR):
            chip = ((z + NEAR - dz) % NEAR) * 8 + ((y + NEAR - dy) % NEAR) * 2
            for q in range(QUARTERS):
                rows = slice(q * PACK, (q + 1) * PACK)
                filt_ref[chip + core, q] = ref[dz, core, rows, :].astype(F32)
                filt_ref[chip + 1 - core, q] = other_ref[dy, dz, rows, :].astype(F32)
    filt_rows = filt_ref.reshape(BLOCKS * QUARTERS * PACK, SIDE)

    def one_batch(batch, carry):
        taps = channels(filt_rows, batch).astype(BF16)
        filt = jnp.dot(first_ref[...], jnp.concatenate([taps, taps], 0), preferred_element_type=F32)
        lhs = rotated(filt, cos_ref[...], sin_ref[...])
        out_ref[pl.ds(batch * BATCH * SIDE, BATCH * SIDE), :] = jnp.dot(lhs, fwd_ref[...], preferred_element_type=F32)
        return carry

    lax.fori_loop(0, PACK // BATCH, one_batch, 0, unroll=UNROLL)


def middle_kernel(in_ref, spectra_ref, first_ref, fwd_ref, inv_ref, last_ref, cos_ref, sin_ref, out_ref, prod_ref, conv_ref):
    rows = BLOCKS * QUARTERS * PACK
    edge = in_ref[:, QUARTERS * PACK :, :].astype(F32)
    scale = edge[:, :, 0:1]
    for q in range(QUARTERS):
        prod_ref[:, q] = decode(in_ref[:, q * PACK : (q + 1) * PACK, :].astype(F32), scale)

    def part(place, i):
        lane = 8 + place * 8 + 2 * i
        return edge[:, :, lane : lane + 1] + edge[:, :, lane + 1 : lane + 2]

    def behind(x):
        return jnp.concatenate([jnp.zeros_like(x[:1]), x[:-1]], 0)

    first = (part(0, 0) + behind(part(0, 2))) * (part(1, 0) + behind(part(1, 2)))
    second = (part(0, 1) + behind(part(0, 3))) * (part(1, 1) + behind(part(1, 3)))
    lane = lax.broadcasted_iota(jnp.int32, (BLOCKS, PACK, SIDE), 2)
    prod_ref[:, 0] = jnp.where(lane == 0, first, jnp.where(lane == 1, second, prod_ref[:, 0]))

    prod_rows = prod_ref.reshape(rows, SIDE)
    conv_rows = conv_ref.reshape(rows, SIDE)

    def one_batch(batch, carry):
        cos, sin = cos_ref[...], sin_ref[...]
        hi, lo = split(channels(prod_rows, batch))
        data = jnp.dot(first_ref[...], jnp.concatenate([hi, lo, hi], 0), preferred_element_type=F32)
        x = jnp.dot(rotated(data, cos, sin), fwd_ref[...], preferred_element_type=F32)
        h = spectra_ref[pl.ds(batch * BATCH * SIDE, BATCH * SIDE), :]
        x_re, x_im, h_re, h_im = x[:, :SIDE], x[:, SIDE:], h[:, :SIDE], h[:, SIDE:]
        hi, lo = split(jnp.concatenate([x_re * h_re - x_im * h_im, x_re * h_im + x_im * h_re], 1))
        back = jnp.dot(jnp.concatenate([hi, lo, hi], 1), inv_ref[...], preferred_element_type=F32)
        cols = []
        for i in range(BATCH):
            re, im = back[i * SIDE : (i + 1) * SIDE, :SIDE], back[i * SIDE : (i + 1) * SIDE, SIDE:]
            cols.append(jnp.concatenate([re * cos - im * sin, im * cos + re * sin], 0))
        hi, lo = split(jnp.concatenate(cols, 1))
        y = jnp.dot(last_ref[...], jnp.concatenate([hi, lo, hi], 0), preferred_element_type=F32)
        for i in range(BATCH):
            conv_rows[pl.ds(BATCH * batch + i, SIDE, stride=PACK), :] = y[:, i * SIDE : (i + 1) * SIDE]
        return carry

    lax.fori_loop(0, PACK // BATCH, one_batch, 0, unroll=UNROLL)

    conv = [conv_ref[:, q] for q in range(QUARTERS)]
    largest = functools.reduce(jnp.maximum, [jnp.abs(c) for c in conv])
    scale = scale_up(jnp.max(largest, axis=2, keepdims=True))
    inverse = 1.0 / scale
    for q in range(QUARTERS):
        out_ref[:, q * PACK : (q + 1) * PACK, :] = encode(conv[q], inverse).astype(BF16)
    out_ref[:, QUARTERS * PACK :, :] = jnp.broadcast_to(scale, (BLOCKS, PACK, SIDE)).astype(BF16)


def end_kernel(query_ref, key_ref, value_ref, halo_ref, taps_ref, gain_ref, conv_ref, out_ref, pad_ref):
    def stream(place, ref):
        return mixed(ref[...].astype(F32), halo_ref[place].astype(F32), taps_ref[place], pad_ref)

    product = stream(1, key_ref) * stream(2, value_ref)
    query = stream(0, query_ref)
    direct = gain_ref[...] * product
    scale = conv_ref[:, QUARTERS * PACK :, 0:1].astype(F32)
    for q in range(QUARTERS):
        conv = decode(conv_ref[:, q * PACK : (q + 1) * PACK, :].astype(F32), scale)
        rows = slice(q * SIDE, (q + 1) * SIDE)
        out_ref[rows, :] = (query[rows] * (conv.reshape(GROUP, SIDE).T + direct[rows])).astype(BF16)


def local(consts, query_input, key_input, value_input, filter_taps, short_taps, skip_gain):
    steps = CHANS // GROUP
    rows_spec = pl.BlockSpec((TOKENS, GROUP), lambda i: (0, i))
    taps_spec = pl.BlockSpec((3, 3, GROUP), lambda i: (0, 0, i))
    params = pltpu.CompilerParams(vmem_limit_bytes=60 * 1024 * 1024)
    small = pltpu.CompilerParams(vmem_limit_bytes=32 * 1024 * 1024)

    last_rows = jnp.stack([query_input[-2:], key_input[-2:], value_input[-2:]])
    pairs = [(i, i + 1) for i in range(BLOCKS - 1)]
    halo = lax.ppermute(last_rows, "seq", pairs)

    def swap(x):
        return lax.all_to_all(x, "seq", split_axis=0, concat_axis=0, tiled=True)

    first, first_exact, fwd, inv, last, cos, sin = [jnp.asarray(c) for c in consts]
    me = lax.axis_index("seq")
    z, y, core = me // 8, (me // 2) % 4, me % 2
    every = range(BLOCKS)
    along_z = [[(i, (i + 8 * d) % 32) for i in every] for d in range(NEAR)]
    along_y = [[(i, i // 8 * 8 + (i + 2 * d) % 8) for i in every] for d in range(NEAR)]

    def filter_for(d):
        part = lax.dynamic_slice_in_dim(filter_taps, (z + d) % NEAR * GROUP, GROUP, 1)
        return lax.ppermute(part, "seq", along_z[d]) if d else part

    turned = pl.pallas_call(
        turn_kernel,
        out_shape=jax.ShapeDtypeStruct((NEAR, NEAR, 2, QUARTERS * PACK, SIDE), BF16),
        compiler_params=small,
        cost_estimate=pl.CostEstimate(flops=10**8, bytes_accessed=2**20, transcendentals=0),
        name="turn",
    )(*[filter_for(d) for d in range(NEAR)])

    def turned_for(d):
        part = lax.dynamic_index_in_dim(turned, (y + d) % NEAR, 0, keepdims=False)
        return lax.ppermute(part, "seq", along_y[d]) if d else part

    bands = [turned_for(d) for d in range(NEAR)]
    to_other = jnp.stack([lax.dynamic_index_in_dim(b, 1 - core, 1, keepdims=False) for b in bands])
    from_other = lax.ppermute(to_other, "seq", [(i, i ^ 1) for i in every])

    product_sent = pl.pallas_call(
        product_kernel,
        grid=(steps,),
        in_specs=[rows_spec, rows_spec, taps_spec],
        cost_estimate=pl.CostEstimate(flops=10**8, bytes_accessed=2**22, transcendentals=0),
        out_specs=pl.BlockSpec((SENDS, OUT_TILES * PACK, SIDE), lambda i: (i, 0, 0)),
        out_shape=jax.ShapeDtypeStruct((BLOCKS, OUT_TILES * PACK, SIDE), BF16),
        scratch_shapes=[pltpu.VMEM((TOKENS + 8, GROUP), F32), pltpu.VMEM((SIDE, GROUP), F32)],
        compiler_params=params,
        name="product",
    )(key_input, value_input, short_taps)
    product_arrived = swap(product_sent)

    work = pltpu.VMEM((BLOCKS, QUARTERS, PACK, SIDE), F32)
    spectra = pl.pallas_call(
        spectrum_kernel,
        out_shape=jax.ShapeDtypeStruct((PACK * SIDE, 2 * SIDE), F32),
        in_specs=[pl.BlockSpec(memory_space=pltpu.SMEM)] + [pl.BlockSpec(memory_space=pltpu.VMEM)] * 9,
        scratch_shapes=[work],
        compiler_params=small,
        cost_estimate=pl.CostEstimate(flops=4 * 10**9, bytes_accessed=4 * 10**6, transcendentals=0),
        name="spectrum",
    )(me.astype(jnp.int32)[None], *bands, from_other, first_exact, fwd, cos, sin)
    conv = pl.pallas_call(
        middle_kernel,
        out_shape=jax.ShapeDtypeStruct((BLOCKS, OUT_TILES * PACK, SIDE), BF16),
        scratch_shapes=[work, work],
        compiler_params=small,
        name="middle",
    )(product_arrived, spectra, first, fwd, inv, last, cos, sin)
    returned = lax.all_to_all(conv, "seq", split_axis=0, concat_axis=0, tiled=True)

    return pl.pallas_call(
        end_kernel,
        grid=(steps,),
        in_specs=[
            rows_spec,
            rows_spec,
            rows_spec,
            pl.BlockSpec((3, 2, GROUP), lambda i: (0, 0, i)),
            taps_spec,
            pl.BlockSpec((1, GROUP), lambda i: (0, i)),
            pl.BlockSpec((SENDS, OUT_TILES * PACK, SIDE), lambda i: (i, 0, 0)),
        ],
        out_specs=rows_spec,
        out_shape=jax.ShapeDtypeStruct((TOKENS, CHANS), BF16),
        scratch_shapes=[pltpu.VMEM((TOKENS + 8, GROUP), F32)],
        compiler_params=small,
        name="end",
    )(query_input, key_input, value_input, halo, short_taps, skip_gain[None, :], returned)


def solution(mesh):
    placed = (
        P("seq", "chan"),
        P("seq", "chan"),
        P("seq", "chan"),
        P("seq", "chan"),
        P(None, None, "chan"),
        P("chan"),
    )
    return jax.shard_map(
        functools.partial(local, tables()),
        mesh=mesh,
        in_specs=placed,
        out_specs=P("seq", "chan"),
        check_vma=False,
    )
```

```python
import functools
import math

import jax
import jax.numpy as jnp
import ml_dtypes
import numpy as np
from jax import lax
from jax.experimental import pallas as pl
from jax.experimental.pallas import tpu as pltpu
from jax.sharding import PartitionSpec as P

F32 = jnp.float32
BF16 = jnp.bfloat16

SIDE = 128
LENGTH = SIDE * SIDE
PACK = 16
BLOCKS = 32
NEAR = 4
TOKENS = 512
CHANS = 512
QUARTERS = TOKENS // SIDE
BATCH = 8
UNROLL = 2
STEP_A, STEP_B, STEP_C, STEP_D = 8, 8, 4, 8
GROUP = 128
OUT_TILES = QUARTERS + 1

SPAN = 252.0
DROP = 125.5
TINY = 1e-35


def split_const(table):
    hi = table.astype(ml_dtypes.bfloat16)
    lo = (table - hi.astype(np.float64)).astype(ml_dtypes.bfloat16)
    return hi, lo


def tables():
    n = np.arange(SIDE, dtype=np.float64)
    ang = 2.0 * np.pi / SIDE * np.outer(n - 0.25, n)
    first = np.concatenate([np.cos(ang), -np.sin(ang)], 0)
    tw = 2.0 * np.pi / LENGTH * np.outer(n - 0.25, n)
    mid = 2.0 * np.pi / SIDE * (np.outer(n, n) % SIDE)
    cos, sin = np.cos(mid), np.sin(mid)
    fwd = np.block([[cos, -sin], [sin, cos]])
    first_hi, first_lo = split_const(first)
    fwd_hi, fwd_lo = split_const(fwd)
    matrices = np.concatenate([np.concatenate([first_hi, first_lo], 1), fwd_hi, fwd_lo], 0)
    return matrices, np.stack([np.cos(tw), np.sin(tw)]).astype(np.float32)


def split(x):
    hi = x.astype(BF16)
    lo = (x - hi.astype(F32)).astype(BF16)
    return hi, lo


def scale_up(largest):
    return jnp.maximum(largest * 1.004, TINY).astype(BF16).astype(F32)


def encode(x, inverse_scale):
    u = jnp.abs(x) * inverse_scale
    y = jnp.exp2(u * lax.rsqrt(jnp.maximum(u, TINY)) * SPAN - DROP)
    return jnp.where(x < 0.0, -y, y)


def decode(y, scale):
    g = (jnp.log2(jnp.abs(y)) + DROP) * (1.0 / SPAN)
    x = g * g * scale
    return jnp.where(y < 0.0, -x, x)


def turn_kernel(*refs):
    *blocks, out_ref = refs
    for i, ref in enumerate(blocks):
        for q in range(QUARTERS):
            block = ref[q * SIDE : (q + 1) * SIDE, :].astype(F32).T.astype(BF16)
            out_ref[:, i, :, q * PACK : (q + 1) * PACK, :] = block.reshape(NEAR, 2, PACK, SIDE)


def product_kernel(key_ref, value_ref, taps_ref, out_hbm, key_pad, value_pad, work_ref, edge_ref, out_ref, out_sems):
    key_pad[0:8, :] = jnp.zeros((8, CHANS), F32)
    value_pad[0:8, :] = jnp.zeros((8, CHANS), F32)

    def mix(pad, place, start):
        return (
            taps_ref[place, 0:1] * pad[pl.ds(8 + start, SIDE), :]
            + taps_ref[place, 1:2] * pad[pl.ds(7 + start, SIDE), :]
            + taps_ref[place, 2:3] * pad[pl.ds(6 + start, SIDE), :]
        )

    largest = jnp.zeros((1, CHANS), F32)
    for q in range(QUARTERS):
        rows = pl.ds(q * SIDE, SIDE)
        key_pad[pl.ds(8 + q * SIDE, SIDE), :] = key_ref[rows, :].astype(F32)
        value_pad[pl.ds(8 + q * SIDE, SIDE), :] = value_ref[rows, :].astype(F32)
        product = mix(key_pad, 1, q * SIDE) * mix(value_pad, 2, q * SIDE)
        work_ref[rows, :] = product
        largest = jnp.maximum(largest, jnp.max(jnp.abs(product), axis=0, keepdims=True))
    scale = scale_up(largest)
    inverse = 1.0 / scale

    out_copies = []

    def put(tile, block):
        rows = pl.ds(tile * PACK, PACK)
        out_ref[:, rows, :] = block.T.astype(BF16).reshape(BLOCKS, PACK, SIDE)
        copy = pltpu.make_async_copy(out_ref.at[:, rows], out_hbm.at[:, rows], out_sems.at[tile])
        copy.start()
        out_copies.append(copy)

    for q in range(QUARTERS):
        put(q, encode(work_ref[pl.ds(q * SIDE, SIDE), :], inverse))

    edge_ref[...] = jnp.zeros_like(edge_ref)
    edge_ref[0:1, :] = scale
    for place, pad in enumerate((key_pad, value_pad)):
        taps = taps_ref[place + 1]
        first, second = pad[8:9, :], pad[9:10, :]
        before, last = pad[TOKENS + 6 : TOKENS + 7, :], pad[TOKENS + 7 : TOKENS + 8, :]
        parts = (
            taps[0:1] * first,
            taps[0:1] * second + taps[1:2] * first,
            taps[1:2] * last + taps[2:3] * before,
            taps[2:3] * last,
        )
        for i, part in enumerate(parts):
            hi, lo = split(part)
            row = 8 + place * 8 + 2 * i
            edge_ref[row : row + 1, :] = hi.astype(F32)
            edge_ref[row + 1 : row + 2, :] = lo.astype(F32)
    put(QUARTERS, edge_ref[...])
    for copy in out_copies:
        copy.wait()


def rotated(block, cos, sin):
    lhs = []
    for i in range(block.shape[1] // SIDE):
        re, im = block[:SIDE, i * SIDE : (i + 1) * SIDE], block[SIDE:, i * SIDE : (i + 1) * SIDE]
        hi, lo = split(jnp.concatenate([re * cos + im * sin, im * cos - re * sin], 1))
        lhs.append(jnp.concatenate([hi, lo, hi], 1))
    return jnp.concatenate(lhs, 0)


def channels(rows, batch):
    return jnp.concatenate([rows[pl.ds(BATCH * batch + i, SIDE, stride=PACK), :] for i in range(BATCH)], 1)


def gather_filter(place_ref, band_refs, other_ref, filt_ref):
    me = place_ref[0]
    z, y, core = me // 8, (me // 2) % 4, me % 2
    for dy, ref in enumerate(band_refs):
        for dz in range(NEAR):
            chip = ((z + NEAR - dz) % NEAR) * 8 + ((y + NEAR - dy) % NEAR) * 2
            for q in range(QUARTERS):
                rows = slice(q * PACK, (q + 1) * PACK)
                filt_ref[chip + core, q] = ref[dz, core, rows, :].astype(F32)
                filt_ref[chip + 1 - core, q] = other_ref[dy, dz, rows, :].astype(F32)


def middle_kernel(
    place_ref, in_ref, b0_ref, b1_ref, b2_ref, b3_ref, other_ref,
    mats_ref, twiddle_ref,
    out_ref, prod_ref, filt_ref, conv_ref,
):
    gather_filter(place_ref, (b0_ref, b1_ref, b2_ref, b3_ref), other_ref, filt_ref)
    rows = BLOCKS * QUARTERS * PACK
    edge = in_ref[:, QUARTERS * PACK :, :].astype(F32)
    scale = edge[:, :, 0:1]
    for q in range(QUARTERS):
        prod_ref[:, q] = decode(in_ref[:, q * PACK : (q + 1) * PACK, :].astype(F32), scale)

    def part(place, i):
        lane = 8 + place * 8 + 2 * i
        return edge[:, :, lane : lane + 1] + edge[:, :, lane + 1 : lane + 2]

    def behind(x):
        return jnp.concatenate([jnp.zeros_like(x[:1]), x[:-1]], 0)

    first = (part(0, 0) + behind(part(0, 2))) * (part(1, 0) + behind(part(1, 2)))
    second = (part(0, 1) + behind(part(0, 3))) * (part(1, 1) + behind(part(1, 3)))
    lane = lax.broadcasted_iota(jnp.int32, (BLOCKS, PACK, SIDE), 2)
    prod_ref[:, 0] = jnp.where(lane == 0, first, jnp.where(lane == 1, second, prod_ref[:, 0]))

    prod_rows = prod_ref.reshape(rows, SIDE)
    filt_rows = filt_ref.reshape(rows, SIDE)
    conv_rows = conv_ref.reshape(rows, SIDE)

    def turned(x):
        return x.astype(F32).T

    two = 2 * SIDE
    first_exact = mats_ref[:two, :]
    first_hi, first_lo = first_exact[:, :SIDE], first_exact[:, SIDE:]
    fwd_hi, fwd_lo = mats_ref[two : 2 * two, :], mats_ref[2 * two :, :]
    inv_hi, inv_lo = turned(fwd_hi).astype(BF16), turned(fwd_lo).astype(BF16)
    last_hi, last_lo = [(turned(x) * (1.0 / LENGTH)).astype(BF16) for x in (first_hi, first_lo)]
    first = jnp.concatenate(
        [jnp.concatenate([first_hi, first_hi], 1), jnp.concatenate([first_lo, jnp.zeros_like(first_lo)], 1)], 0
    )
    fwd = jnp.concatenate([fwd_hi, fwd_hi, fwd_lo], 0)
    inv = jnp.concatenate([inv_hi, inv_hi, inv_lo], 0)
    last = jnp.concatenate([last_hi, last_lo], 0)

    def dot(left, right):
        return jnp.dot(left, right, preferred_element_type=F32)

    def by_rows(left, right, step):
        return jnp.concatenate([dot(left[i : i + step * SIDE], right) for i in range(0, BATCH * SIDE, step * SIDE)], 0)

    def by_columns(left, right, step):
        return jnp.concatenate([dot(left, right[:, i : i + step * SIDE]) for i in range(0, BATCH * SIDE, step * SIDE)], 1)

    def one_batch(batch, carry):
        cos, sin = twiddle_ref[0], twiddle_ref[1]
        hi, lo = split(channels(prod_rows, batch))
        data = by_columns(first, jnp.concatenate([hi, lo], 0), STEP_A)
        data = data[:two] + data[two:]
        taps = channels(filt_rows, batch).astype(BF16)
        filt = by_columns(first_exact, jnp.concatenate([taps, taps], 0), STEP_A)
        x = by_rows(rotated(data, cos, sin), fwd, STEP_B)
        h = by_rows(rotated(filt, cos, sin), fwd, STEP_B)
        x_re, x_im, h_re, h_im = x[:, :SIDE], x[:, SIDE:], h[:, :SIDE], h[:, SIDE:]
        hi, lo = split(jnp.concatenate([x_re * h_re - x_im * h_im, x_re * h_im + x_im * h_re], 1))
        back = by_rows(jnp.concatenate([hi, lo, hi], 1), inv, STEP_C)
        cols = []
        for i in range(BATCH):
            re, im = back[i * SIDE : (i + 1) * SIDE, :SIDE], back[i * SIDE : (i + 1) * SIDE, SIDE:]
            cols.append(jnp.concatenate([re * cos - im * sin, im * cos + re * sin], 0))
        hi, lo = split(jnp.concatenate(cols, 1))
        y = by_columns(last, hi, STEP_D)
        y = y[:SIDE] + y[SIDE:] + by_columns(last_hi, lo, STEP_D)
        for i in range(BATCH):
            conv_rows[pl.ds(BATCH * batch + i, SIDE, stride=PACK), :] = y[:, i * SIDE : (i + 1) * SIDE]
        return carry

    lax.fori_loop(0, PACK // BATCH, one_batch, 0, unroll=UNROLL)

    conv = [conv_ref[:, q] for q in range(QUARTERS)]
    largest = functools.reduce(jnp.maximum, [jnp.abs(c) for c in conv])
    scale = scale_up(jnp.max(largest, axis=2, keepdims=True))
    inverse = 1.0 / scale
    for q in range(QUARTERS):
        out_ref[:, q * PACK : (q + 1) * PACK, :] = encode(conv[q], inverse).astype(BF16)
    out_ref[:, QUARTERS * PACK :, :] = jnp.broadcast_to(scale, (BLOCKS, PACK, SIDE)).astype(BF16)


def end_kernel(query_ref, key_ref, value_ref, halo_ref, taps_ref, gain_ref, conv_ref, out_hbm, query_pad, key_pad, value_pad, out_ref, sems):
    pads = (query_pad, key_pad, value_pad)
    for place, pad in enumerate(pads):
        pad[6:8, :] = halo_ref[place].astype(F32)

    def mix(place, ref, start):
        pad, taps = pads[place], taps_ref[place]
        pad[pl.ds(8 + start, SIDE), :] = ref[pl.ds(start, SIDE), :].astype(F32)
        return (
            taps[0:1] * pad[pl.ds(8 + start, SIDE), :]
            + taps[1:2] * pad[pl.ds(7 + start, SIDE), :]
            + taps[2:3] * pad[pl.ds(6 + start, SIDE), :]
        )

    scale = conv_ref[:, QUARTERS * PACK :, 0:1].astype(F32)
    copies = []
    for q in range(QUARTERS):
        start = q * SIDE
        rows = pl.ds(start, SIDE)
        conv = decode(conv_ref[:, q * PACK : (q + 1) * PACK, :].astype(F32), scale)
        direct = gain_ref[...] * (mix(1, key_ref, start) * mix(2, value_ref, start))
        out_ref[rows, :] = (mix(0, query_ref, start) * (conv.reshape(CHANS, SIDE).T + direct)).astype(BF16)
        copy = pltpu.make_async_copy(out_ref.at[rows], out_hbm.at[rows], sems.at[q])
        copy.start()
        copies.append(copy)
    for copy in copies:
        copy.wait()


def local(consts, query_input, key_input, value_input, filter_taps, short_taps, skip_gain):
    small = pltpu.CompilerParams(vmem_limit_bytes=32 * 1024 * 1024)

    last_rows = jnp.stack([query_input[-2:], key_input[-2:], value_input[-2:]])
    pairs = [(i, i + 1) for i in range(BLOCKS - 1)]
    halo = lax.ppermute(last_rows, "seq", pairs)

    def swap(x):
        return lax.all_to_all(x, "seq", split_axis=0, concat_axis=0, tiled=True)

    me = lax.axis_index("seq")
    z, y, core = me // 8, (me // 2) % 4, me % 2
    every = range(BLOCKS)
    along_z = [[(i, (i + 8 * d) % 32) for i in every] for d in range(NEAR)]
    along_y = [[(i, i // 8 * 8 + (i + 2 * d) % 8) for i in every] for d in range(NEAR)]

    def filter_for(d):
        part = lax.dynamic_slice_in_dim(filter_taps, (z + d) % NEAR * GROUP, GROUP, 1)
        return lax.ppermute(part, "seq", along_z[d]) if d else part

    turned = pl.pallas_call(
        turn_kernel,
        out_shape=jax.ShapeDtypeStruct((NEAR, NEAR, 2, QUARTERS * PACK, SIDE), BF16),
        compiler_params=small,
        cost_estimate=pl.CostEstimate(flops=2 * 10**10, bytes_accessed=2**20, transcendentals=0),
        name="turn",
    )(*[filter_for(d) for d in range(NEAR)])

    def turned_for(d):
        part = lax.dynamic_index_in_dim(turned, (y + d) % NEAR, 0, keepdims=False)
        return lax.ppermute(part, "seq", along_y[d]) if d else part

    bands = [turned_for(d) for d in range(NEAR)]
    to_other = jnp.stack([lax.dynamic_index_in_dim(b, 1 - core, 1, keepdims=False) for b in bands])
    from_other = lax.ppermute(to_other, "seq", [(i, i ^ 1) for i in every])

    hbm = pl.BlockSpec(memory_space=pl.ANY)
    vmem = pl.BlockSpec(memory_space=pltpu.VMEM)
    product_sent = pl.pallas_call(
        product_kernel,
        in_specs=[vmem, vmem, vmem],
        out_specs=hbm,
        out_shape=jax.ShapeDtypeStruct((BLOCKS, OUT_TILES * PACK, SIDE), BF16),
        scratch_shapes=[
            pltpu.VMEM((TOKENS + 8, CHANS), F32),
            pltpu.VMEM((TOKENS + 8, CHANS), F32),
            pltpu.VMEM((TOKENS, CHANS), F32),
            pltpu.VMEM((SIDE, CHANS), F32),
            pltpu.VMEM((BLOCKS, OUT_TILES * PACK, SIDE), BF16),
            pltpu.SemaphoreType.DMA((OUT_TILES,)),
        ],
        compiler_params=small,
        cost_estimate=pl.CostEstimate(flops=2 * 10**10, bytes_accessed=2**22, transcendentals=0),
        name="product",
    )(key_input, value_input, short_taps)
    product_arrived = swap(product_sent)

    work = pltpu.VMEM((BLOCKS, QUARTERS, PACK, SIDE), F32)
    conv = pl.pallas_call(
        middle_kernel,
        out_shape=jax.ShapeDtypeStruct((BLOCKS, OUT_TILES * PACK, SIDE), BF16),
        in_specs=[pl.BlockSpec(memory_space=pltpu.SMEM)] + [pl.BlockSpec(memory_space=pltpu.VMEM)] * 8,
        scratch_shapes=[work, work, work],
        compiler_params=small,
        cost_estimate=pl.CostEstimate(flops=8 * 10**9, bytes_accessed=2 * 10**6, transcendentals=0),
        name="middle",
    )(me.astype(jnp.int32)[None], product_arrived, *bands, from_other, *[jnp.asarray(c) for c in consts])
    returned = lax.all_to_all(conv, "seq", split_axis=0, concat_axis=0, tiled=True)

    pad = pltpu.VMEM((TOKENS + 8, CHANS), F32)
    return pl.pallas_call(
        end_kernel,
        in_specs=[vmem] * 7,
        out_specs=hbm,
        out_shape=jax.ShapeDtypeStruct((TOKENS, CHANS), BF16),
        scratch_shapes=[pad, pad, pad, pltpu.VMEM((TOKENS, CHANS), BF16), pltpu.SemaphoreType.DMA((QUARTERS,))],
        compiler_params=small,
        name="end",
    )(query_input, key_input, value_input, halo, short_taps, skip_gain[None, :], returned)


def solution(mesh):
    placed = (
        P("seq", "chan"),
        P("seq", "chan"),
        P("seq", "chan"),
        P("seq", "chan"),
        P(None, None, "chan"),
        P("chan"),
    )
    return jax.shard_map(
        functools.partial(local, tables()),
        mesh=mesh,
        in_specs=placed,
        out_specs=P("seq", "chan"),
        check_vma=False,
    )
```

```python
import functools
import math

import jax
import jax.numpy as jnp
import ml_dtypes
import numpy as np
from jax import lax
from jax.experimental import pallas as pl
from jax.experimental.pallas import tpu as pltpu
from jax.sharding import PartitionSpec as P

F32 = jnp.float32
BF16 = jnp.bfloat16

SIDE = 128
LENGTH = SIDE * SIDE
PACK = 16
BLOCKS = 32
NEAR = 4
TOKENS = 512
CHANS = 512
QUARTERS = TOKENS // SIDE
BATCH = 8
STEP_A, STEP_B, STEP_C, STEP_D = 8, 8, 4, 8
GROUP = 128
HALF_ROWS = QUARTERS * PACK // 2
OUT_TILES = QUARTERS + 1

SPAN = 252.0
DROP = 125.5
TINY = 1e-35


def split_const(table):
    hi = table.astype(ml_dtypes.bfloat16)
    lo = (table - hi.astype(np.float64)).astype(ml_dtypes.bfloat16)
    return hi, lo


def tables():
    n = np.arange(SIDE, dtype=np.float64)
    ang = 2.0 * np.pi / SIDE * np.outer(n - 0.25, n)
    first = np.concatenate([np.cos(ang), -np.sin(ang)], 0)
    tw = 2.0 * np.pi / LENGTH * np.outer(n - 0.25, n)
    mid = 2.0 * np.pi / SIDE * (np.outer(n, n) % SIDE)
    cos, sin = np.cos(mid), np.sin(mid)
    fwd = np.block([[cos, -sin], [sin, cos]])
    first_hi, first_lo = split_const(first)
    fwd_hi, fwd_lo = split_const(fwd)
    matrices = np.concatenate([np.concatenate([first_hi, first_lo], 1), fwd_hi, fwd_lo], 0)
    return matrices, np.stack([np.cos(tw), np.sin(tw)]).astype(np.float32)


def split(x):
    hi = x.astype(BF16)
    lo = (x - hi.astype(F32)).astype(BF16)
    return hi, lo


def scale_up(largest):
    return jnp.maximum(largest * 1.004, TINY).astype(BF16).astype(F32)


def encode(x, inverse_scale):
    u = jnp.abs(x) * inverse_scale
    y = jnp.exp2(u * lax.rsqrt(jnp.maximum(u, TINY)) * SPAN - DROP)
    return jnp.where(x < 0.0, -y, y)


def decode(y, scale):
    g = (jnp.log2(jnp.abs(y)) + DROP) * (1.0 / SPAN)
    x = g * g * scale
    return jnp.where(y < 0.0, -x, x)


def turn_kernel(*refs):
    *blocks, out_ref = refs
    for i, ref in enumerate(blocks):
        for q in range(QUARTERS):
            block = ref[q * SIDE : (q + 1) * SIDE, :].astype(F32).T.astype(BF16)
            out_ref[:, i, :, q * PACK : (q + 1) * PACK, :] = block.reshape(NEAR, 2, PACK, SIDE)


def product_kernel(key_ref, value_ref, taps_ref, out_ref, key_pad, value_pad, work_ref, edge_ref):
    key_pad[0:8, :] = jnp.zeros((8, CHANS), F32)
    value_pad[0:8, :] = jnp.zeros((8, CHANS), F32)

    def mix(pad, place, start):
        return (
            taps_ref[place, 0:1] * pad[pl.ds(8 + start, SIDE), :]
            + taps_ref[place, 1:2] * pad[pl.ds(7 + start, SIDE), :]
            + taps_ref[place, 2:3] * pad[pl.ds(6 + start, SIDE), :]
        )

    largest = jnp.zeros((1, CHANS), F32)
    for q in range(QUARTERS):
        rows = pl.ds(q * SIDE, SIDE)
        key_pad[pl.ds(8 + q * SIDE, SIDE), :] = key_ref[rows, :].astype(F32)
        value_pad[pl.ds(8 + q * SIDE, SIDE), :] = value_ref[rows, :].astype(F32)
        product = mix(key_pad, 1, q * SIDE) * mix(value_pad, 2, q * SIDE)
        work_ref[rows, :] = product
        largest = jnp.maximum(largest, jnp.max(jnp.abs(product), axis=0, keepdims=True))
    scale = scale_up(largest)
    inverse = 1.0 / scale

    def put(tile, block):
        rows = pl.ds(tile * PACK, PACK)
        out_ref[:, rows, :] = block.T.astype(BF16).reshape(BLOCKS, PACK, SIDE)

    for q in range(QUARTERS):
        put(q, encode(work_ref[pl.ds(q * SIDE, SIDE), :], inverse))

    edge_ref[...] = jnp.zeros_like(edge_ref)
    edge_ref[0:1, :] = scale
    for place, pad in enumerate((key_pad, value_pad)):
        taps = taps_ref[place + 1]
        first, second = pad[8:9, :], pad[9:10, :]
        before, last = pad[TOKENS + 6 : TOKENS + 7, :], pad[TOKENS + 7 : TOKENS + 8, :]
        parts = (
            taps[0:1] * first,
            taps[0:1] * second + taps[1:2] * first,
            taps[1:2] * last + taps[2:3] * before,
            taps[2:3] * last,
        )
        for i, part in enumerate(parts):
            hi, lo = split(part)
            row = 8 + place * 8 + 2 * i
            edge_ref[row : row + 1, :] = hi.astype(F32)
            edge_ref[row + 1 : row + 2, :] = lo.astype(F32)
    put(QUARTERS, edge_ref[...])


def pick_kernel(*refs):
    *blocks, out_ref = refs
    for i, ref in enumerate(blocks):
        out_ref[:, i] = ref[...].reshape(NEAR, 2, HALF_ROWS, SIDE)


def rotated(block, cos, sin):
    lhs = []
    for i in range(block.shape[1] // SIDE):
        re, im = block[:SIDE, i * SIDE : (i + 1) * SIDE], block[SIDE:, i * SIDE : (i + 1) * SIDE]
        hi, lo = split(jnp.concatenate([re * cos + im * sin, im * cos - re * sin], 1))
        lhs.append(jnp.concatenate([hi, lo, hi], 1))
    return jnp.concatenate(lhs, 0)


def channels(rows, batch):
    return jnp.concatenate([rows[pl.ds(BATCH * batch + i, SIDE, stride=PACK), :] for i in range(BATCH)], 1)


def gather_filter(place_ref, band_refs, other_ref, filt_ref):
    me = place_ref[0]
    z, y, core = me // 8, (me // 2) % 4, me % 2
    for dy, ref in enumerate(band_refs):
        for dz in range(NEAR):
            chip = ((z + NEAR - dz) % NEAR) * 8 + ((y + NEAR - dy) % NEAR) * 2
            for q in range(QUARTERS):
                rows = slice(q * PACK, (q + 1) * PACK)
                filt_ref[chip + core, q] = ref[dz, core, rows, :].astype(F32)
                filt_ref[chip + 1 - core, q] = other_ref[dy, dz, rows, :].astype(F32)


def middle_kernel(
    place_ref, in_ref, b0_ref, b1_ref, b2_ref, b3_ref, other_ref,
    mats_ref, twiddle_ref,
    out_ref, hops_ref, prod_ref, filt_ref, conv_ref,
):
    gather_filter(place_ref, (b0_ref, b1_ref, b2_ref, b3_ref), other_ref, filt_ref)
    rows = BLOCKS * QUARTERS * PACK
    edge = in_ref[:, QUARTERS * PACK :, :].astype(F32)

    def behind(x):
        return jnp.concatenate([jnp.zeros_like(x[:1]), x[:-1]], 0)

    lane = lax.broadcasted_iota(jnp.int32, (BLOCKS, BATCH, SIDE), 2)

    def decode_batch(batch):
        some = slice(batch * BATCH, (batch + 1) * BATCH)
        side = edge[:, some]
        scale = side[:, :, 0:1]

        def part(place, i):
            at = 8 + place * 8 + 2 * i
            return side[:, :, at : at + 1] + side[:, :, at + 1 : at + 2]

        first = (part(0, 0) + behind(part(0, 2))) * (part(1, 0) + behind(part(1, 2)))
        second = (part(0, 1) + behind(part(0, 3))) * (part(1, 1) + behind(part(1, 3)))
        for q in range(QUARTERS):
            x = decode(in_ref[:, q * PACK : (q + 1) * PACK, :].astype(F32)[:, some], scale)
            if q == 0:
                x = jnp.where(lane == 0, first, jnp.where(lane == 1, second, x))
            prod_ref[:, q, some] = x

    prod_rows = prod_ref.reshape(rows, SIDE)
    filt_rows = filt_ref.reshape(rows, SIDE)
    conv_rows = conv_ref.reshape(rows, SIDE)

    def turned(x):
        return x.astype(F32).T

    two = 2 * SIDE
    first_exact = mats_ref[:two, :]
    first_hi, first_lo = first_exact[:, :SIDE], first_exact[:, SIDE:]
    fwd_hi, fwd_lo = mats_ref[two : 2 * two, :], mats_ref[2 * two :, :]
    inv_hi, inv_lo = turned(fwd_hi).astype(BF16), turned(fwd_lo).astype(BF16)
    last_hi, last_lo = [(turned(x) * (1.0 / LENGTH)).astype(BF16) for x in (first_hi, first_lo)]
    first = jnp.concatenate(
        [jnp.concatenate([first_hi, first_hi], 1), jnp.concatenate([first_lo, jnp.zeros_like(first_lo)], 1)], 0
    )
    fwd = jnp.concatenate([fwd_hi, fwd_hi, fwd_lo], 0)
    inv = jnp.concatenate([inv_hi, inv_hi, inv_lo], 0)
    last = jnp.concatenate([last_hi, last_lo], 0)

    def dot(left, right):
        return jnp.dot(left, right, preferred_element_type=F32)

    def by_rows(left, right, step):
        return jnp.concatenate([dot(left[i : i + step * SIDE], right) for i in range(0, BATCH * SIDE, step * SIDE)], 0)

    def by_columns(left, right, step):
        return jnp.concatenate([dot(left, right[:, i : i + step * SIDE]) for i in range(0, BATCH * SIDE, step * SIDE)], 1)

    cos, sin = twiddle_ref[0], twiddle_ref[1]

    def filter_spectra(batch):
        taps = channels(filt_rows, batch).astype(BF16)
        filt = by_columns(first_exact, jnp.concatenate([taps, taps], 0), STEP_A)
        return by_rows(rotated(filt, cos, sin), fwd, STEP_B)

    def data_spectra(batch):
        hi, lo = split(channels(prod_rows, batch))
        data = by_columns(first, jnp.concatenate([hi, lo], 0), STEP_A)
        return by_rows(rotated(data[:two] + data[two:], cos, sin), fwd, STEP_B)

    def back(batch, x, h):
        x_re, x_im, h_re, h_im = x[:, :SIDE], x[:, SIDE:], h[:, :SIDE], h[:, SIDE:]
        hi, lo = split(jnp.concatenate([x_re * h_re - x_im * h_im, x_re * h_im + x_im * h_re], 1))
        back = by_rows(jnp.concatenate([hi, lo, hi], 1), inv, STEP_C)
        cols = []
        for i in range(BATCH):
            re, im = back[i * SIDE : (i + 1) * SIDE, :SIDE], back[i * SIDE : (i + 1) * SIDE, SIDE:]
            cols.append(jnp.concatenate([re * cos - im * sin, im * cos + re * sin], 0))
        hi, lo = split(jnp.concatenate(cols, 1))
        y = by_columns(last, hi, STEP_D)
        y = y[:SIDE] + y[SIDE:] + by_columns(last_hi, lo, STEP_D)
        for i in range(BATCH):
            conv_rows[pl.ds(BATCH * batch + i, SIDE, stride=PACK), :] = y[:, i * SIDE : (i + 1) * SIDE]

    scales = []

    def encode_batch(batch):
        some = slice(batch * BATCH, (batch + 1) * BATCH)
        conv = [conv_ref[:, q, some] for q in range(QUARTERS)]
        largest = functools.reduce(jnp.maximum, [jnp.abs(c) for c in conv])
        scale = scale_up(jnp.max(largest, axis=2, keepdims=True))
        inverse = 1.0 / scale
        for q in range(QUARTERS):
            conv_ref[:, q, some] = encode(conv[q], inverse)
        scales.append(scale)

    h0 = filter_spectra(0)
    h1 = filter_spectra(1)
    decode_batch(0)
    x0 = data_spectra(0)
    decode_batch(1)
    x1 = data_spectra(1)
    back(0, x0, h0)
    back(1, x1, h1)
    encode_batch(0)
    encode_batch(1)
    for batch, ref in enumerate((out_ref, hops_ref)):
        some = slice(batch * BATCH, (batch + 1) * BATCH)
        for p in range(QUARTERS // 2):
            both = jnp.concatenate([conv_ref[:, 2 * p, some], conv_ref[:, 2 * p + 1, some]], 1)
            ref[:, p * PACK : (p + 1) * PACK, :] = both.astype(BF16)
    scale = jnp.concatenate(scales, 1)
    out_ref[:, HALF_ROWS:, :] = jnp.broadcast_to(scale, (BLOCKS, PACK, SIDE)).astype(BF16)


def gate_kernel(query_hbm, key_hbm, value_hbm, halo_ref, taps_ref, gain_ref, picked_hbm, mix_ref, direct_ref, rows_ref, query_pad, key_pad, value_pad, sems):
    pads = (query_pad, key_pad, value_pad)
    copies = []
    for place, hbm in enumerate((query_hbm, key_hbm, value_hbm)):
        copy = pltpu.make_async_copy(hbm, rows_ref.at[place], sems.at[place])
        copy.start()
        copies.append(copy)
    for place, pad in enumerate(pads):
        pad[6:8, :] = halo_ref[place].astype(F32)
        copies[place].wait()

    def mix(place, start):
        pad, taps = pads[place], taps_ref[place]
        pad[pl.ds(8 + start, SIDE), :] = rows_ref[place, pl.ds(start, SIDE), :].astype(F32)
        return (
            taps[0:1] * pad[pl.ds(8 + start, SIDE), :]
            + taps[1:2] * pad[pl.ds(7 + start, SIDE), :]
            + taps[2:3] * pad[pl.ds(6 + start, SIDE), :]
        )

    for q in range(QUARTERS):
        start = q * SIDE
        query = mix(0, start)
        mix_ref[pl.ds(start, SIDE), :] = query
        direct_ref[pl.ds(start, SIDE), :] = query * (gain_ref[...] * (mix(1, start) * mix(2, start)))


def other_kernel(place_ref, b0_ref, b1_ref, b2_ref, b3_ref, ready_hbm, out_ref):
    core = place_ref[0] % 2
    for dy, ref in enumerate((b0_ref, b1_ref, b2_ref, b3_ref)):
        out_ref[dy] = ref[:, 1 - core]


def end_kernel(place_ref, mix_ref, direct_ref, conv_ref, b0_ref, b1_ref, b2_ref, b3_ref, other_ref, out_hbm, hops_ref, out_ref, sems):
    me = place_ref[0]
    z, y, core = me // 8, (me // 2) % 4, me % 2
    for dy, ref in enumerate((b0_ref, b1_ref, b2_ref, b3_ref)):
        for dz in range(NEAR):
            chip = ((z + NEAR - dz) % NEAR) * 8 + ((y + NEAR - dy) % NEAR) * 2
            hops_ref[chip + core] = ref[dz, core]
            hops_ref[chip + 1 - core] = other_ref[dy, dz]
    scale = conv_ref[:, HALF_ROWS:, 0:1].astype(F32)
    copies = []
    for p in range(QUARTERS // 2):
        tile = slice(p * PACK, (p + 1) * PACK)
        near, far = conv_ref[:, tile, :].astype(F32), hops_ref[:, tile, :].astype(F32)
        for i in range(2):
            some = slice(i * BATCH, (i + 1) * BATCH)
            conv = decode(jnp.concatenate([near[:, some], far[:, some]], 1), scale).reshape(CHANS, SIDE).T
            rows = pl.ds((2 * p + i) * SIDE, SIDE)
            out_ref[rows, :] = (mix_ref[rows, :] * conv + direct_ref[rows, :]).astype(BF16)
            copy = pltpu.make_async_copy(out_ref.at[rows], out_hbm.at[rows], sems.at[2 * p + i])
            copy.start()
            copies.append(copy)
    for copy in copies:
        copy.wait()


def local(consts, query_input, key_input, value_input, filter_taps, short_taps, skip_gain):
    small = pltpu.CompilerParams(vmem_limit_bytes=32 * 1024 * 1024)

    last_rows = jnp.stack([query_input[-2:], key_input[-2:], value_input[-2:]])
    pairs = [(i, i + 1) for i in range(BLOCKS - 1)]
    halo = lax.ppermute(last_rows, "seq", pairs)

    def swap(x):
        return lax.all_to_all(x, "seq", split_axis=0, concat_axis=0, tiled=True)

    me = lax.axis_index("seq")
    z, y, core = me // 8, (me // 2) % 4, me % 2
    every = range(BLOCKS)
    along_z = [[(i, (i + 8 * d) % 32) for i in every] for d in range(NEAR)]
    along_y = [[(i, i // 8 * 8 + (i + 2 * d) % 8) for i in every] for d in range(NEAR)]

    def filter_for(d):
        part = lax.dynamic_slice_in_dim(filter_taps, (z + d) % NEAR * GROUP, GROUP, 1)
        return lax.ppermute(part, "seq", along_z[d]) if d else part

    turned = pl.pallas_call(
        turn_kernel,
        out_shape=jax.ShapeDtypeStruct((NEAR, NEAR, 2, QUARTERS * PACK, SIDE), BF16),
        compiler_params=small,
        cost_estimate=pl.CostEstimate(flops=2 * 10**10, bytes_accessed=2**20, transcendentals=0),
        name="turn",
    )(*[filter_for(d) for d in range(NEAR)])

    def turned_for(d):
        part = lax.dynamic_index_in_dim(turned, (y + d) % NEAR, 0, keepdims=False)
        return lax.ppermute(part, "seq", along_y[d]) if d else part

    bands = [turned_for(d) for d in range(NEAR)]
    hbm = pl.BlockSpec(memory_space=pl.ANY)
    vmem = pl.BlockSpec(memory_space=pltpu.VMEM)
    smem = pl.BlockSpec(memory_space=pltpu.SMEM)
    place = me.astype(jnp.int32)[None]

    def for_other(blocks, ready):
        return pl.pallas_call(
            other_kernel,
            in_specs=[smem] + [vmem] * 4 + [hbm],
            out_shape=jax.ShapeDtypeStruct((NEAR, NEAR, *blocks[0].shape[2:]), BF16),
            compiler_params=small,
            name="other",
        )(place, *blocks, ready)

    to_other = for_other(bands, halo)
    from_other = lax.ppermute(to_other, "seq", [(i, i ^ 1) for i in every])

    product_sent = pl.pallas_call(
        product_kernel,
        in_specs=[vmem, vmem, vmem],
        out_specs=vmem,
        out_shape=jax.ShapeDtypeStruct((BLOCKS, OUT_TILES * PACK, SIDE), BF16),
        scratch_shapes=[
            pltpu.VMEM((TOKENS + 8, CHANS), F32),
            pltpu.VMEM((TOKENS + 8, CHANS), F32),
            pltpu.VMEM((TOKENS, CHANS), F32),
            pltpu.VMEM((SIDE, CHANS), F32),
        ],
        compiler_params=small,
        cost_estimate=pl.CostEstimate(flops=2 * 10**10, bytes_accessed=2**22, transcendentals=0),
        name="product",
    )(key_input, value_input, short_taps)
    product_arrived = swap(product_sent)

    work = pltpu.VMEM((BLOCKS, QUARTERS, PACK, SIDE), F32)
    conv, hops = pl.pallas_call(
        middle_kernel,
        in_specs=[smem] + [vmem] * 8,
        out_shape=[
            jax.ShapeDtypeStruct((BLOCKS, HALF_ROWS + PACK, SIDE), BF16),
            jax.ShapeDtypeStruct((BLOCKS, HALF_ROWS, SIDE), BF16),
        ],
        scratch_shapes=[work, work, work],
        compiler_params=small,
        cost_estimate=pl.CostEstimate(flops=8 * 10**9, bytes_accessed=2 * 10**6, transcendentals=0),
        name="middle",
    )(place, product_arrived, *bands, from_other, *[jnp.asarray(c) for c in consts])

    def conv_for(d):
        part = lax.dynamic_slice_in_dim(hops, (z + d) % NEAR * 8, 8, 0)
        return lax.ppermute(part, "seq", along_z[d]) if d else part

    picked = pl.pallas_call(
        pick_kernel,
        out_shape=jax.ShapeDtypeStruct((NEAR, NEAR, 2, HALF_ROWS, SIDE), BF16),
        compiler_params=small,
        cost_estimate=pl.CostEstimate(flops=2 * 10**10, bytes_accessed=2**20, transcendentals=0),
        name="pick",
    )(*[conv_for(d) for d in range(NEAR)])

    def picked_for(d):
        part = lax.dynamic_index_in_dim(picked, (y + d) % NEAR, 0, keepdims=False)
        return lax.ppermute(part, "seq", along_y[d]) if d else part

    returned = swap(conv)
    conv_bands = [picked_for(d) for d in range(NEAR)]
    pad = pltpu.VMEM((TOKENS + 8, CHANS), F32)
    query_mix, direct = pl.pallas_call(
        gate_kernel,
        in_specs=[hbm] * 3 + [vmem] * 3 + [hbm],
        out_shape=[jax.ShapeDtypeStruct((TOKENS, CHANS), F32)] * 2,
        scratch_shapes=[pltpu.VMEM((3, TOKENS, CHANS), BF16), pad, pad, pad, pltpu.SemaphoreType.DMA((3,))],
        compiler_params=small,
        cost_estimate=pl.CostEstimate(flops=10**9, bytes_accessed=4 * 10**6, transcendentals=0),
        name="gate",
    )(query_input, key_input, value_input, halo, short_taps, skip_gain[None, :], picked)
    conv_to_other = for_other(conv_bands, direct)
    conv_from_other = lax.ppermute(conv_to_other, "seq", [(i, i ^ 1) for i in every])
    return pl.pallas_call(
        end_kernel,
        in_specs=[smem] + [vmem] * 8,
        out_specs=hbm,
        out_shape=jax.ShapeDtypeStruct((TOKENS, CHANS), BF16),
        scratch_shapes=[
            pltpu.VMEM((BLOCKS, HALF_ROWS, SIDE), BF16),
            pltpu.VMEM((TOKENS, CHANS), BF16),
            pltpu.SemaphoreType.DMA((QUARTERS,)),
        ],
        compiler_params=small,
        name="end",
    )(place, query_mix, direct, returned, *conv_bands, conv_from_other)


def solution(mesh):
    placed = (
        P("seq", "chan"),
        P("seq", "chan"),
        P("seq", "chan"),
        P("seq", "chan"),
        P(None, None, "chan"),
        P("chan"),
    )
    return jax.shard_map(
        functools.partial(local, tables()),
        mesh=mesh,
        in_specs=placed,
        out_specs=P("seq", "chan"),
        check_vma=False,
    )
```

```python
import functools
import math

import jax
import jax.numpy as jnp
import ml_dtypes
import numpy as np
from jax import lax
from jax.experimental import pallas as pl
from jax.experimental.pallas import tpu as pltpu
from jax.sharding import PartitionSpec as P

F32 = jnp.float32
BF16 = jnp.bfloat16

SIDE = 128
LENGTH = SIDE * SIDE
PACK = 16
BLOCKS = 32
NEAR = 4
TURN_ORDER = (0, 2, 3, 1)
TOKENS = 512
CHANS = 512
QUARTERS = TOKENS // SIDE
BATCH = 8
STEP_A, STEP_B, STEP_C, STEP_D = 8, 8, 4, 8
GROUP = 128
HALF_ROWS = QUARTERS * PACK // 2
OUT_TILES = QUARTERS + 1

SPAN = 252.0
DROP = 125.5
TINY = 1e-35


def split_const(table):
    hi = table.astype(ml_dtypes.bfloat16)
    lo = (table - hi.astype(np.float64)).astype(ml_dtypes.bfloat16)
    return hi, lo


def tables():
    n = np.arange(SIDE, dtype=np.float64)
    ang = 2.0 * np.pi / SIDE * np.outer(n - 0.25, n)
    first = np.concatenate([np.cos(ang), -np.sin(ang)], 0)
    tw = 2.0 * np.pi / LENGTH * np.outer(n - 0.25, n)
    mid = 2.0 * np.pi / SIDE * (np.outer(n, n) % SIDE)
    cos, sin = np.cos(mid), np.sin(mid)
    fwd = np.block([[cos, -sin], [sin, cos]])
    first_hi, first_lo = split_const(first)
    fwd_hi, fwd_lo = split_const(fwd)
    matrices = np.concatenate([np.concatenate([first_hi, first_lo], 1), fwd_hi, fwd_lo], 0)
    return matrices, np.stack([np.cos(tw), np.sin(tw)]).astype(np.float32)


def split(x):
    hi = x.astype(BF16)
    lo = (x - hi.astype(F32)).astype(BF16)
    return hi, lo


def scale_up(largest):
    return jnp.maximum(largest * 1.004, TINY).astype(BF16).astype(F32)


def encode(x, inverse_scale):
    u = jnp.abs(x) * inverse_scale
    y = jnp.exp2(u * lax.rsqrt(jnp.maximum(u, TINY)) * SPAN - DROP)
    return jnp.where(x < 0.0, -y, y)


def decode(y, scale):
    g = (jnp.log2(jnp.abs(y)) + DROP) * (1.0 / SPAN)
    x = g * g * scale
    return jnp.where(y < 0.0, -x, x)


def turn_kernel(*refs):
    *blocks, out_ref = refs
    for i, ref in zip(TURN_ORDER, blocks):
        for q in range(QUARTERS):
            block = ref[q * SIDE : (q + 1) * SIDE, :].astype(F32).T.astype(BF16)
            out_ref[:, i, :, q * PACK : (q + 1) * PACK, :] = block.reshape(NEAR, 2, PACK, SIDE)


def product_kernel(key_ref, value_ref, taps_ref, out_ref, key_pad, value_pad, work_ref, edge_ref):
    key_pad[0:8, :] = jnp.zeros((8, CHANS), F32)
    value_pad[0:8, :] = jnp.zeros((8, CHANS), F32)

    def mix(pad, place, start):
        return (
            taps_ref[place, 0:1] * pad[pl.ds(8 + start, SIDE), :]
            + taps_ref[place, 1:2] * pad[pl.ds(7 + start, SIDE), :]
            + taps_ref[place, 2:3] * pad[pl.ds(6 + start, SIDE), :]
        )

    largest = jnp.zeros((1, CHANS), F32)
    for q in range(QUARTERS):
        rows = pl.ds(q * SIDE, SIDE)
        key_pad[pl.ds(8 + q * SIDE, SIDE), :] = key_ref[rows, :].astype(F32)
        value_pad[pl.ds(8 + q * SIDE, SIDE), :] = value_ref[rows, :].astype(F32)
        product = mix(key_pad, 1, q * SIDE) * mix(value_pad, 2, q * SIDE)
        work_ref[rows, :] = product
        largest = jnp.maximum(largest, jnp.max(jnp.abs(product), axis=0, keepdims=True))
    scale = scale_up(largest)
    inverse = 1.0 / scale

    def put(tile, block):
        rows = pl.ds(tile * PACK, PACK)
        out_ref[:, rows, :] = block.T.astype(BF16).reshape(BLOCKS, PACK, SIDE)

    for q in range(QUARTERS):
        put(q, encode(work_ref[pl.ds(q * SIDE, SIDE), :], inverse))

    edge_ref[...] = jnp.zeros_like(edge_ref)
    edge_ref[0:1, :] = scale
    for place, pad in enumerate((key_pad, value_pad)):
        taps = taps_ref[place + 1]
        first, second = pad[8:9, :], pad[9:10, :]
        before, last = pad[TOKENS + 6 : TOKENS + 7, :], pad[TOKENS + 7 : TOKENS + 8, :]
        parts = (
            taps[0:1] * first,
            taps[0:1] * second + taps[1:2] * first,
            taps[1:2] * last + taps[2:3] * before,
            taps[2:3] * last,
        )
        for i, part in enumerate(parts):
            hi, lo = split(part)
            row = 8 + place * 8 + 2 * i
            edge_ref[row : row + 1, :] = hi.astype(F32)
            edge_ref[row + 1 : row + 2, :] = lo.astype(F32)
    put(QUARTERS, edge_ref[...])


def pick_kernel(*refs):
    *blocks, out_ref = refs
    for i, ref in enumerate(blocks):
        out_ref[:, i] = ref[...].reshape(NEAR, 2, HALF_ROWS, SIDE)


def rotated(block, cos, sin):
    lhs = []
    for i in range(block.shape[1] // SIDE):
        re, im = block[:SIDE, i * SIDE : (i + 1) * SIDE], block[SIDE:, i * SIDE : (i + 1) * SIDE]
        hi, lo = split(jnp.concatenate([re * cos + im * sin, im * cos - re * sin], 1))
        lhs.append(jnp.concatenate([hi, lo, hi], 1))
    return jnp.concatenate(lhs, 0)


def channels(rows, batch):
    return jnp.concatenate([rows[pl.ds(BATCH * batch + i, SIDE, stride=PACK), :] for i in range(BATCH)], 1)


def gather_filter(place_ref, band_refs, other_ref, filt_ref):
    me = place_ref[0]
    z, y, core = me // 8, (me // 2) % 4, me % 2
    for dy, ref in enumerate(band_refs):
        for dz in range(NEAR):
            chip = ((z + NEAR - dz) % NEAR) * 8 + ((y + NEAR - dy) % NEAR) * 2
            for q in range(QUARTERS):
                rows = slice(q * PACK, (q + 1) * PACK)
                filt_ref[chip + core, q] = ref[dz, core, rows, :].astype(F32)
                filt_ref[chip + 1 - core, q] = other_ref[dy, dz, rows, :].astype(F32)


def middle_kernel(
    place_ref, in_ref, b0_ref, b1_ref, b2_ref, b3_ref, other_ref,
    mats_ref, twiddle_ref,
    out_ref, hops_ref, prod_ref, filt_ref, conv_ref,
):
    gather_filter(place_ref, (b0_ref, b1_ref, b2_ref, b3_ref), other_ref, filt_ref)
    rows = BLOCKS * QUARTERS * PACK
    edge = in_ref[:, QUARTERS * PACK :, :].astype(F32)

    def behind(x):
        return jnp.concatenate([jnp.zeros_like(x[:1]), x[:-1]], 0)

    lane = lax.broadcasted_iota(jnp.int32, (BLOCKS, BATCH, SIDE), 2)

    def decode_batch(batch):
        some = slice(batch * BATCH, (batch + 1) * BATCH)
        side = edge[:, some]
        scale = side[:, :, 0:1]

        def part(place, i):
            at = 8 + place * 8 + 2 * i
            return side[:, :, at : at + 1] + side[:, :, at + 1 : at + 2]

        first = (part(0, 0) + behind(part(0, 2))) * (part(1, 0) + behind(part(1, 2)))
        second = (part(0, 1) + behind(part(0, 3))) * (part(1, 1) + behind(part(1, 3)))
        for q in range(QUARTERS):
            x = decode(in_ref[:, q * PACK : (q + 1) * PACK, :].astype(F32)[:, some], scale)
            if q == 0:
                x = jnp.where(lane == 0, first, jnp.where(lane == 1, second, x))
            prod_ref[:, q, some] = x

    prod_rows = prod_ref.reshape(rows, SIDE)
    filt_rows = filt_ref.reshape(rows, SIDE)
    conv_rows = conv_ref.reshape(rows, SIDE)

    def turned(x):
        return x.astype(F32).T

    two = 2 * SIDE
    first_exact = mats_ref[:two, :]
    first_hi, first_lo = first_exact[:, :SIDE], first_exact[:, SIDE:]
    fwd_hi, fwd_lo = mats_ref[two : 2 * two, :], mats_ref[2 * two :, :]
    inv_hi, inv_lo = turned(fwd_hi).astype(BF16), turned(fwd_lo).astype(BF16)
    last_hi, last_lo = [(turned(x) * (1.0 / LENGTH)).astype(BF16) for x in (first_hi, first_lo)]
    first = jnp.concatenate(
        [jnp.concatenate([first_hi, first_hi], 1), jnp.concatenate([first_lo, jnp.zeros_like(first_lo)], 1)], 0
    )
    fwd = jnp.concatenate([fwd_hi, fwd_hi, fwd_lo], 0)
    inv = jnp.concatenate([inv_hi, inv_hi, inv_lo], 0)
    last = jnp.concatenate([last_hi, last_lo], 0)

    def dot(left, right):
        return jnp.dot(left, right, preferred_element_type=F32)

    def by_rows(left, right, step):
        return jnp.concatenate([dot(left[i : i + step * SIDE], right) for i in range(0, BATCH * SIDE, step * SIDE)], 0)

    def by_columns(left, right, step):
        return jnp.concatenate([dot(left, right[:, i : i + step * SIDE]) for i in range(0, BATCH * SIDE, step * SIDE)], 1)

    cos, sin = twiddle_ref[0], twiddle_ref[1]

    def filter_spectra(batch):
        taps = channels(filt_rows, batch).astype(BF16)
        filt = by_columns(first_exact, jnp.concatenate([taps, taps], 0), STEP_A)
        return by_rows(rotated(filt, cos, sin), fwd, STEP_B)

    def data_spectra(batch):
        hi, lo = split(channels(prod_rows, batch))
        data = by_columns(first, jnp.concatenate([hi, lo], 0), STEP_A)
        return by_rows(rotated(data[:two] + data[two:], cos, sin), fwd, STEP_B)

    def back(batch, x, h):
        x_re, x_im, h_re, h_im = x[:, :SIDE], x[:, SIDE:], h[:, :SIDE], h[:, SIDE:]
        hi, lo = split(jnp.concatenate([x_re * h_re - x_im * h_im, x_re * h_im + x_im * h_re], 1))
        back = by_rows(jnp.concatenate([hi, lo, hi], 1), inv, STEP_C)
        cols = []
        for i in range(BATCH):
            re, im = back[i * SIDE : (i + 1) * SIDE, :SIDE], back[i * SIDE : (i + 1) * SIDE, SIDE:]
            cols.append(jnp.concatenate([re * cos - im * sin, im * cos + re * sin], 0))
        hi, lo = split(jnp.concatenate(cols, 1))
        y = by_columns(last, hi, STEP_D)
        y = y[:SIDE] + y[SIDE:] + by_columns(last_hi, lo, STEP_D)
        for i in range(BATCH):
            conv_rows[pl.ds(BATCH * batch + i, SIDE, stride=PACK), :] = y[:, i * SIDE : (i + 1) * SIDE]

    scales = []

    def encode_batch(batch):
        some = slice(batch * BATCH, (batch + 1) * BATCH)
        conv = [conv_ref[:, q, some] for q in range(QUARTERS)]
        largest = functools.reduce(jnp.maximum, [jnp.abs(c) for c in conv])
        scale = scale_up(jnp.max(largest, axis=2, keepdims=True))
        inverse = 1.0 / scale
        for q in range(QUARTERS):
            conv_ref[:, q, some] = encode(conv[q], inverse)
        scales.append(scale)

    h0 = filter_spectra(0)
    h1 = filter_spectra(1)
    decode_batch(0)
    x0 = data_spectra(0)
    decode_batch(1)
    x1 = data_spectra(1)
    back(0, x0, h0)
    back(1, x1, h1)
    encode_batch(0)
    encode_batch(1)
    for batch, ref in enumerate((out_ref, hops_ref)):
        some = slice(batch * BATCH, (batch + 1) * BATCH)
        for p in range(QUARTERS // 2):
            both = jnp.concatenate([conv_ref[:, 2 * p, some], conv_ref[:, 2 * p + 1, some]], 1)
            ref[:, p * PACK : (p + 1) * PACK, :] = both.astype(BF16)
    scale = jnp.concatenate(scales, 1)
    out_ref[:, HALF_ROWS:, :] = jnp.broadcast_to(scale, (BLOCKS, PACK, SIDE)).astype(BF16)


def gate_kernel(query_hbm, key_hbm, value_hbm, halo_ref, taps_ref, gain_ref, picked_hbm, mix_ref, direct_ref, rows_ref, query_pad, key_pad, value_pad, sems):
    pads = (query_pad, key_pad, value_pad)
    copies = []
    for place, hbm in enumerate((query_hbm, key_hbm, value_hbm)):
        copy = pltpu.make_async_copy(hbm, rows_ref.at[place], sems.at[place])
        copy.start()
        copies.append(copy)
    for place, pad in enumerate(pads):
        pad[6:8, :] = halo_ref[place].astype(F32)
        copies[place].wait()

    def mix(place, start):
        pad, taps = pads[place], taps_ref[place]
        pad[pl.ds(8 + start, SIDE), :] = rows_ref[place, pl.ds(start, SIDE), :].astype(F32)
        return (
            taps[0:1] * pad[pl.ds(8 + start, SIDE), :]
            + taps[1:2] * pad[pl.ds(7 + start, SIDE), :]
            + taps[2:3] * pad[pl.ds(6 + start, SIDE), :]
        )

    for q in range(QUARTERS):
        start = q * SIDE
        query = mix(0, start)
        mix_ref[pl.ds(start, SIDE), :] = query
        direct_ref[pl.ds(start, SIDE), :] = query * (gain_ref[...] * (mix(1, start) * mix(2, start)))


def other_kernel(place_ref, b0_ref, b1_ref, b2_ref, b3_ref, ready_hbm, out_ref):
    core = place_ref[0] % 2
    for dy, ref in enumerate((b0_ref, b1_ref, b2_ref, b3_ref)):
        out_ref[dy] = ref[:, 1 - core]


def end_kernel(place_ref, mix_ref, direct_ref, conv_ref, b0_ref, b1_ref, b2_ref, b3_ref, other_ref, out_hbm, hops_ref, out_ref, sems):
    me = place_ref[0]
    z, y, core = me // 8, (me // 2) % 4, me % 2
    for dy, ref in enumerate((b0_ref, b1_ref, b2_ref, b3_ref)):
        for dz in range(NEAR):
            chip = ((z + NEAR - dz) % NEAR) * 8 + ((y + NEAR - dy) % NEAR) * 2
            hops_ref[chip + core] = ref[dz, core]
            hops_ref[chip + 1 - core] = other_ref[dy, dz]
    scale = conv_ref[:, HALF_ROWS:, 0:1].astype(F32)
    copies = []
    for p in range(QUARTERS // 2):
        tile = slice(p * PACK, (p + 1) * PACK)
        near, far = conv_ref[:, tile, :].astype(F32), hops_ref[:, tile, :].astype(F32)
        for i in range(2):
            some = slice(i * BATCH, (i + 1) * BATCH)
            conv = decode(jnp.concatenate([near[:, some], far[:, some]], 1), scale).reshape(CHANS, SIDE).T
            rows = pl.ds((2 * p + i) * SIDE, SIDE)
            out_ref[rows, :] = (mix_ref[rows, :] * conv + direct_ref[rows, :]).astype(BF16)
            copy = pltpu.make_async_copy(out_ref.at[rows], out_hbm.at[rows], sems.at[2 * p + i])
            copy.start()
            copies.append(copy)
    for copy in copies:
        copy.wait()


def local(consts, query_input, key_input, value_input, filter_taps, short_taps, skip_gain):
    small = pltpu.CompilerParams(vmem_limit_bytes=32 * 1024 * 1024)

    last_rows = jnp.stack([query_input[-2:], key_input[-2:], value_input[-2:]])
    pairs = [(i, i + 1) for i in range(BLOCKS - 1)]
    halo = lax.ppermute(last_rows, "seq", pairs)

    def swap(x):
        return lax.all_to_all(x, "seq", split_axis=0, concat_axis=0, tiled=True)

    me = lax.axis_index("seq")
    z, y, core = me // 8, (me // 2) % 4, me % 2
    every = range(BLOCKS)
    along_z = [[(i, (i + 8 * d) % 32) for i in every] for d in range(NEAR)]
    along_y = [[(i, i // 8 * 8 + (i + 2 * d) % 8) for i in every] for d in range(NEAR)]

    def filter_for(d):
        part = lax.dynamic_slice_in_dim(filter_taps, (z + d) % NEAR * GROUP, GROUP, 1)
        return lax.ppermute(part, "seq", along_z[d]) if d else part

    turned = pl.pallas_call(
        turn_kernel,
        out_shape=jax.ShapeDtypeStruct((NEAR, NEAR, 2, QUARTERS * PACK, SIDE), BF16),
        compiler_params=small,
        cost_estimate=pl.CostEstimate(flops=2 * 10**10, bytes_accessed=2**20, transcendentals=0),
        name="turn",
    )(*[filter_for(d) for d in TURN_ORDER])

    def turned_for(d):
        part = lax.dynamic_index_in_dim(turned, (y + d) % NEAR, 0, keepdims=False)
        return lax.ppermute(part, "seq", along_y[d]) if d else part

    bands = [turned_for(d) for d in range(NEAR)]
    hbm = pl.BlockSpec(memory_space=pl.ANY)
    vmem = pl.BlockSpec(memory_space=pltpu.VMEM)
    smem = pl.BlockSpec(memory_space=pltpu.SMEM)
    place = me.astype(jnp.int32)[None]

    def for_other(blocks, ready):
        return pl.pallas_call(
            other_kernel,
            in_specs=[smem] + [vmem] * 4 + [hbm],
            out_shape=jax.ShapeDtypeStruct((NEAR, NEAR, *blocks[0].shape[2:]), BF16),
            compiler_params=small,
            name="other",
        )(place, *blocks, ready)

    to_other = for_other(bands, halo)
    from_other = lax.ppermute(to_other, "seq", [(i, i ^ 1) for i in every])

    product_sent = pl.pallas_call(
        product_kernel,
        in_specs=[vmem, vmem, vmem],
        out_specs=vmem,
        out_shape=jax.ShapeDtypeStruct((BLOCKS, OUT_TILES * PACK, SIDE), BF16),
        scratch_shapes=[
            pltpu.VMEM((TOKENS + 8, CHANS), F32),
            pltpu.VMEM((TOKENS + 8, CHANS), F32),
            pltpu.VMEM((TOKENS, CHANS), F32),
            pltpu.VMEM((SIDE, CHANS), F32),
        ],
        compiler_params=small,
        cost_estimate=pl.CostEstimate(flops=2 * 10**10, bytes_accessed=2**22, transcendentals=0),
        name="product",
    )(key_input, value_input, short_taps)
    product_arrived = swap(product_sent)

    work = pltpu.VMEM((BLOCKS, QUARTERS, PACK, SIDE), F32)
    conv, hops = pl.pallas_call(
        middle_kernel,
        in_specs=[smem] + [vmem] * 8,
        out_shape=[
            jax.ShapeDtypeStruct((BLOCKS, HALF_ROWS + PACK, SIDE), BF16),
            jax.ShapeDtypeStruct((BLOCKS, HALF_ROWS, SIDE), BF16),
        ],
        scratch_shapes=[work, work, work],
        compiler_params=small,
        cost_estimate=pl.CostEstimate(flops=8 * 10**9, bytes_accessed=2 * 10**6, transcendentals=0),
        name="middle",
    )(place, product_arrived, *bands, from_other, *[jnp.asarray(c) for c in consts])

    def conv_for(d):
        part = lax.dynamic_slice_in_dim(hops, (z + d) % NEAR * 8, 8, 0)
        return lax.ppermute(part, "seq", along_z[d]) if d else part

    picked = pl.pallas_call(
        pick_kernel,
        out_shape=jax.ShapeDtypeStruct((NEAR, NEAR, 2, HALF_ROWS, SIDE), BF16),
        compiler_params=small,
        cost_estimate=pl.CostEstimate(flops=2 * 10**10, bytes_accessed=2**20, transcendentals=0),
        name="pick",
    )(*[conv_for(d) for d in range(NEAR)])

    def picked_for(d):
        part = lax.dynamic_index_in_dim(picked, (y + d) % NEAR, 0, keepdims=False)
        return lax.ppermute(part, "seq", along_y[d]) if d else part

    returned = swap(conv)
    conv_bands = [picked_for(d) for d in range(NEAR)]
    pad = pltpu.VMEM((TOKENS + 8, CHANS), F32)
    query_mix, direct = pl.pallas_call(
        gate_kernel,
        in_specs=[hbm] * 3 + [vmem] * 3 + [hbm],
        out_shape=[jax.ShapeDtypeStruct((TOKENS, CHANS), F32)] * 2,
        scratch_shapes=[pltpu.VMEM((3, TOKENS, CHANS), BF16), pad, pad, pad, pltpu.SemaphoreType.DMA((3,))],
        compiler_params=small,
        cost_estimate=pl.CostEstimate(flops=10**9, bytes_accessed=4 * 10**6, transcendentals=0),
        name="gate",
    )(query_input, key_input, value_input, halo, short_taps, skip_gain[None, :], picked)
    conv_to_other = for_other(conv_bands, direct)
    conv_from_other = lax.ppermute(conv_to_other, "seq", [(i, i ^ 1) for i in every])
    return pl.pallas_call(
        end_kernel,
        in_specs=[smem] + [vmem] * 8,
        out_specs=hbm,
        out_shape=jax.ShapeDtypeStruct((TOKENS, CHANS), BF16),
        scratch_shapes=[
            pltpu.VMEM((BLOCKS, HALF_ROWS, SIDE), BF16),
            pltpu.VMEM((TOKENS, CHANS), BF16),
            pltpu.SemaphoreType.DMA((QUARTERS,)),
        ],
        compiler_params=small,
        name="end",
    )(place, query_mix, direct, returned, *conv_bands, conv_from_other)


def solution(mesh):
    placed = (
        P("seq", "chan"),
        P("seq", "chan"),
        P("seq", "chan"),
        P("seq", "chan"),
        P(None, None, "chan"),
        P("chan"),
    )
    return jax.shard_map(
        functools.partial(local, tables()),
        mesh=mesh,
        in_specs=placed,
        out_specs=P("seq", "chan"),
        check_vma=False,
    )
```

```python
import functools
import math

import jax
import jax.numpy as jnp
import ml_dtypes
import numpy as np
from jax import lax
from jax.experimental import pallas as pl
from jax.experimental.pallas import tpu as pltpu
from jax.sharding import PartitionSpec as P

F32 = jnp.float32
BF16 = jnp.bfloat16

SIDE = 128
LENGTH = SIDE * SIDE
PACK = 16
BLOCKS = 32
NEAR = 4
TURN_ORDER = (0, 2, 3, 1)
BAND_ORDER = (0, 3, 2, 1)
TOKENS = 512
CHANS = 512
QUARTERS = TOKENS // SIDE
BATCH = 8
STEP_A, STEP_B, STEP_C, STEP_D = 8, 8, 4, 8
GROUP = 128
HALF_ROWS = QUARTERS * PACK // 2
OUT_TILES = QUARTERS + 1

SPAN = 252.0
DROP = 125.5
TINY = 1e-35


def split_const(table):
    hi = table.astype(ml_dtypes.bfloat16)
    lo = (table - hi.astype(np.float64)).astype(ml_dtypes.bfloat16)
    return hi, lo


def tables():
    n = np.arange(SIDE, dtype=np.float64)
    ang = 2.0 * np.pi / SIDE * np.outer(n - 0.25, n)
    first = np.concatenate([np.cos(ang), -np.sin(ang)], 0)
    tw = 2.0 * np.pi / LENGTH * np.outer(n - 0.25, n)
    mid = 2.0 * np.pi / SIDE * (np.outer(n, n) % SIDE)
    cos, sin = np.cos(mid), np.sin(mid)
    fwd = np.block([[cos, -sin], [sin, cos]])
    first_hi, first_lo = split_const(first)
    fwd_hi, fwd_lo = split_const(fwd)
    matrices = np.concatenate([np.concatenate([first_hi, first_lo], 1), fwd_hi, fwd_lo], 0)
    return matrices, np.stack([np.cos(tw), np.sin(tw)]).astype(np.float32)


def split(x):
    hi = x.astype(BF16)
    lo = (x - hi.astype(F32)).astype(BF16)
    return hi, lo


def scale_up(largest):
    return jnp.maximum(largest * 1.004, TINY).astype(BF16).astype(F32)


def encode(x, inverse_scale):
    u = jnp.abs(x) * inverse_scale
    y = jnp.exp2(u * lax.rsqrt(jnp.maximum(u, TINY)) * SPAN - DROP)
    return jnp.where(x < 0.0, -y, y)


def decode(y, scale):
    g = (jnp.log2(jnp.abs(y)) + DROP) * (1.0 / SPAN)
    x = g * g * scale
    return jnp.where(y < 0.0, -x, x)


def turn_kernel(*refs):
    *blocks, out_ref = refs
    for i, ref in zip(TURN_ORDER, blocks):
        for q in range(QUARTERS):
            block = ref[q * SIDE : (q + 1) * SIDE, :].astype(F32).T.astype(BF16)
            out_ref[:, i, :, q * PACK : (q + 1) * PACK, :] = block.reshape(NEAR, 2, PACK, SIDE)


def product_kernel(key_ref, value_ref, taps_ref, out_ref, key_pad, value_pad, work_ref, edge_ref):
    key_pad[0:8, :] = jnp.zeros((8, CHANS), F32)
    value_pad[0:8, :] = jnp.zeros((8, CHANS), F32)

    def mix(pad, place, start):
        return (
            taps_ref[place, 0:1] * pad[pl.ds(8 + start, SIDE), :]
            + taps_ref[place, 1:2] * pad[pl.ds(7 + start, SIDE), :]
            + taps_ref[place, 2:3] * pad[pl.ds(6 + start, SIDE), :]
        )

    largest = jnp.zeros((1, CHANS), F32)
    for q in range(QUARTERS):
        rows = pl.ds(q * SIDE, SIDE)
        key_pad[pl.ds(8 + q * SIDE, SIDE), :] = key_ref[rows, :].astype(F32)
        value_pad[pl.ds(8 + q * SIDE, SIDE), :] = value_ref[rows, :].astype(F32)
        product = mix(key_pad, 1, q * SIDE) * mix(value_pad, 2, q * SIDE)
        work_ref[rows, :] = product
        largest = jnp.maximum(largest, jnp.max(jnp.abs(product), axis=0, keepdims=True))
    scale = scale_up(largest)
    inverse = 1.0 / scale

    def put(tile, block):
        rows = pl.ds(tile * PACK, PACK)
        out_ref[:, rows, :] = block.T.astype(BF16).reshape(BLOCKS, PACK, SIDE)

    for q in range(QUARTERS):
        put(q, encode(work_ref[pl.ds(q * SIDE, SIDE), :], inverse))

    edge_ref[...] = jnp.zeros_like(edge_ref)
    edge_ref[0:1, :] = scale
    for place, pad in enumerate((key_pad, value_pad)):
        taps = taps_ref[place + 1]
        first, second = pad[8:9, :], pad[9:10, :]
        before, last = pad[TOKENS + 6 : TOKENS + 7, :], pad[TOKENS + 7 : TOKENS + 8, :]
        parts = (
            taps[0:1] * first,
            taps[0:1] * second + taps[1:2] * first,
            taps[1:2] * last + taps[2:3] * before,
            taps[2:3] * last,
        )
        for i, part in enumerate(parts):
            hi, lo = split(part)
            row = 8 + place * 8 + 2 * i
            edge_ref[row : row + 1, :] = hi.astype(F32)
            edge_ref[row + 1 : row + 2, :] = lo.astype(F32)
    put(QUARTERS, edge_ref[...])


def pick_kernel(*refs):
    *blocks, out_ref = refs
    for i, ref in enumerate(blocks):
        out_ref[:, i] = ref[...].reshape(NEAR, 2, HALF_ROWS, SIDE)


def rotated(block, cos, sin):
    lhs = []
    for i in range(block.shape[1] // SIDE):
        re, im = block[:SIDE, i * SIDE : (i + 1) * SIDE], block[SIDE:, i * SIDE : (i + 1) * SIDE]
        hi, lo = split(jnp.concatenate([re * cos + im * sin, im * cos - re * sin], 1))
        lhs.append(jnp.concatenate([hi, lo, hi], 1))
    return jnp.concatenate(lhs, 0)


def channels(rows, batch):
    return jnp.concatenate([rows[pl.ds(BATCH * batch + i, SIDE, stride=PACK), :] for i in range(BATCH)], 1)


def gather_filter(place_ref, band_refs, other_ref, filt_ref):
    me = place_ref[0]
    z, y, core = me // 8, (me // 2) % 4, me % 2
    for dy, ref in zip(BAND_ORDER, band_refs):
        for dz in range(NEAR):
            chip = ((z + NEAR - dz) % NEAR) * 8 + ((y + NEAR - dy) % NEAR) * 2
            for q in range(QUARTERS):
                rows = slice(q * PACK, (q + 1) * PACK)
                filt_ref[chip + core, q] = ref[dz, core, rows, :].astype(F32)
                filt_ref[chip + 1 - core, q] = other_ref[dy, dz, rows, :].astype(F32)


def middle_kernel(
    place_ref, in_ref, b0_ref, b1_ref, b2_ref, b3_ref, other_ref,
    mats_ref, twiddle_ref,
    out_ref, hops_ref, prod_ref, filt_ref, conv_ref,
):
    gather_filter(place_ref, (b0_ref, b1_ref, b2_ref, b3_ref), other_ref, filt_ref)
    rows = BLOCKS * QUARTERS * PACK
    edge = in_ref[:, QUARTERS * PACK :, :].astype(F32)

    def behind(x):
        return jnp.concatenate([jnp.zeros_like(x[:1]), x[:-1]], 0)

    lane = lax.broadcasted_iota(jnp.int32, (BLOCKS, BATCH, SIDE), 2)

    def decode_batch(batch):
        some = slice(batch * BATCH, (batch + 1) * BATCH)
        side = edge[:, some]
        scale = side[:, :, 0:1]

        def part(place, i):
            at = 8 + place * 8 + 2 * i
            return side[:, :, at : at + 1] + side[:, :, at + 1 : at + 2]

        first = (part(0, 0) + behind(part(0, 2))) * (part(1, 0) + behind(part(1, 2)))
        second = (part(0, 1) + behind(part(0, 3))) * (part(1, 1) + behind(part(1, 3)))
        for q in range(QUARTERS):
            x = decode(in_ref[:, q * PACK : (q + 1) * PACK, :].astype(F32)[:, some], scale)
            if q == 0:
                x = jnp.where(lane == 0, first, jnp.where(lane == 1, second, x))
            prod_ref[:, q, some] = x

    prod_rows = prod_ref.reshape(rows, SIDE)
    filt_rows = filt_ref.reshape(rows, SIDE)
    conv_rows = conv_ref.reshape(rows, SIDE)

    def turned(x):
        return x.astype(F32).T

    two = 2 * SIDE
    first_exact = mats_ref[:two, :]
    first_hi, first_lo = first_exact[:, :SIDE], first_exact[:, SIDE:]
    fwd_hi, fwd_lo = mats_ref[two : 2 * two, :], mats_ref[2 * two :, :]
    inv_hi, inv_lo = turned(fwd_hi).astype(BF16), turned(fwd_lo).astype(BF16)
    last_hi, last_lo = [(turned(x) * (1.0 / LENGTH)).astype(BF16) for x in (first_hi, first_lo)]
    first = jnp.concatenate(
        [jnp.concatenate([first_hi, first_hi], 1), jnp.concatenate([first_lo, jnp.zeros_like(first_lo)], 1)], 0
    )
    fwd = jnp.concatenate([fwd_hi, fwd_hi, fwd_lo], 0)
    inv = jnp.concatenate([inv_hi, inv_hi, inv_lo], 0)
    last = jnp.concatenate([last_hi, last_lo], 0)

    def dot(left, right):
        return jnp.dot(left, right, preferred_element_type=F32)

    def by_rows(left, right, step):
        return jnp.concatenate([dot(left[i : i + step * SIDE], right) for i in range(0, BATCH * SIDE, step * SIDE)], 0)

    def by_columns(left, right, step):
        return jnp.concatenate([dot(left, right[:, i : i + step * SIDE]) for i in range(0, BATCH * SIDE, step * SIDE)], 1)

    cos, sin = twiddle_ref[0], twiddle_ref[1]

    def filter_spectra(batch):
        taps = channels(filt_rows, batch).astype(BF16)
        filt = by_columns(first_exact, jnp.concatenate([taps, taps], 0), STEP_A)
        return by_rows(rotated(filt, cos, sin), fwd, STEP_B)

    def data_spectra(batch):
        hi, lo = split(channels(prod_rows, batch))
        data = by_columns(first, jnp.concatenate([hi, lo], 0), STEP_A)
        return by_rows(rotated(data[:two] + data[two:], cos, sin), fwd, STEP_B)

    def back(batch, x, h):
        x_re, x_im, h_re, h_im = x[:, :SIDE], x[:, SIDE:], h[:, :SIDE], h[:, SIDE:]
        hi, lo = split(jnp.concatenate([x_re * h_re - x_im * h_im, x_re * h_im + x_im * h_re], 1))
        back = by_rows(jnp.concatenate([hi, lo, hi], 1), inv, STEP_C)
        cols = []
        for i in range(BATCH):
            re, im = back[i * SIDE : (i + 1) * SIDE, :SIDE], back[i * SIDE : (i + 1) * SIDE, SIDE:]
            cols.append(jnp.concatenate([re * cos - im * sin, im * cos + re * sin], 0))
        hi, lo = split(jnp.concatenate(cols, 1))
        y = by_columns(last, hi, STEP_D)
        y = y[:SIDE] + y[SIDE:] + by_columns(last_hi, lo, STEP_D)
        for i in range(BATCH):
            conv_rows[pl.ds(BATCH * batch + i, SIDE, stride=PACK), :] = y[:, i * SIDE : (i + 1) * SIDE]

    scales = []

    def encode_batch(batch):
        some = slice(batch * BATCH, (batch + 1) * BATCH)
        conv = [conv_ref[:, q, some] for q in range(QUARTERS)]
        largest = functools.reduce(jnp.maximum, [jnp.abs(c) for c in conv])
        scale = scale_up(jnp.max(largest, axis=2, keepdims=True))
        inverse = 1.0 / scale
        for q in range(QUARTERS):
            conv_ref[:, q, some] = encode(conv[q], inverse)
        scales.append(scale)

    h0 = filter_spectra(0)
    h1 = filter_spectra(1)
    decode_batch(0)
    x0 = data_spectra(0)
    decode_batch(1)
    x1 = data_spectra(1)
    back(0, x0, h0)
    back(1, x1, h1)
    encode_batch(0)
    encode_batch(1)
    for batch, ref in enumerate((out_ref, hops_ref)):
        some = slice(batch * BATCH, (batch + 1) * BATCH)
        for p in range(QUARTERS // 2):
            both = jnp.concatenate([conv_ref[:, 2 * p, some], conv_ref[:, 2 * p + 1, some]], 1)
            ref[:, p * PACK : (p + 1) * PACK, :] = both.astype(BF16)
    scale = jnp.concatenate(scales, 1)
    out_ref[:, HALF_ROWS:, :] = jnp.broadcast_to(scale, (BLOCKS, PACK, SIDE)).astype(BF16)


def gate_kernel(query_hbm, key_hbm, value_hbm, halo_ref, taps_ref, gain_ref, picked_hbm, mix_ref, direct_ref, rows_ref, query_pad, key_pad, value_pad, sems):
    pads = (query_pad, key_pad, value_pad)
    copies = []
    for place, hbm in enumerate((query_hbm, key_hbm, value_hbm)):
        copy = pltpu.make_async_copy(hbm, rows_ref.at[place], sems.at[place])
        copy.start()
        copies.append(copy)
    for place, pad in enumerate(pads):
        pad[6:8, :] = halo_ref[place].astype(F32)
        copies[place].wait()

    def mix(place, start):
        pad, taps = pads[place], taps_ref[place]
        pad[pl.ds(8 + start, SIDE), :] = rows_ref[place, pl.ds(start, SIDE), :].astype(F32)
        return (
            taps[0:1] * pad[pl.ds(8 + start, SIDE), :]
            + taps[1:2] * pad[pl.ds(7 + start, SIDE), :]
            + taps[2:3] * pad[pl.ds(6 + start, SIDE), :]
        )

    for q in range(QUARTERS):
        start = q * SIDE
        query = mix(0, start)
        mix_ref[pl.ds(start, SIDE), :] = query
        direct_ref[pl.ds(start, SIDE), :] = query * (gain_ref[...] * (mix(1, start) * mix(2, start)))


def other_kernel(place_ref, b0_ref, b1_ref, b2_ref, b3_ref, ready_hbm, out_ref):
    core = place_ref[0] % 2
    for dy, ref in zip(BAND_ORDER, (b0_ref, b1_ref, b2_ref, b3_ref)):
        out_ref[dy] = ref[:, 1 - core]


def end_kernel(place_ref, mix_ref, direct_ref, conv_ref, b0_ref, b1_ref, b2_ref, b3_ref, other_ref, out_hbm, hops_ref, out_ref, sems):
    me = place_ref[0]
    z, y, core = me // 8, (me // 2) % 4, me % 2
    for dy, ref in zip(BAND_ORDER, (b0_ref, b1_ref, b2_ref, b3_ref)):
        for dz in range(NEAR):
            chip = ((z + NEAR - dz) % NEAR) * 8 + ((y + NEAR - dy) % NEAR) * 2
            hops_ref[chip + core] = ref[dz, core]
            hops_ref[chip + 1 - core] = other_ref[dy, dz]
    scale = conv_ref[:, HALF_ROWS:, 0:1].astype(F32)
    copies = []
    for p in range(QUARTERS // 2):
        tile = slice(p * PACK, (p + 1) * PACK)
        near, far = conv_ref[:, tile, :].astype(F32), hops_ref[:, tile, :].astype(F32)
        for i in range(2):
            some = slice(i * BATCH, (i + 1) * BATCH)
            conv = decode(jnp.concatenate([near[:, some], far[:, some]], 1), scale).reshape(CHANS, SIDE).T
            rows = pl.ds((2 * p + i) * SIDE, SIDE)
            out_ref[rows, :] = (mix_ref[rows, :] * conv + direct_ref[rows, :]).astype(BF16)
            copy = pltpu.make_async_copy(out_ref.at[rows], out_hbm.at[rows], sems.at[2 * p + i])
            copy.start()
            copies.append(copy)
    for copy in copies:
        copy.wait()


def local(consts, query_input, key_input, value_input, filter_taps, short_taps, skip_gain):
    small = pltpu.CompilerParams(vmem_limit_bytes=32 * 1024 * 1024)

    last_rows = jnp.stack([query_input[-2:], key_input[-2:], value_input[-2:]])
    pairs = [(i, i + 1) for i in range(BLOCKS - 1)]
    halo = lax.ppermute(last_rows, "seq", pairs)

    def swap(x):
        return lax.all_to_all(x, "seq", split_axis=0, concat_axis=0, tiled=True)

    me = lax.axis_index("seq")
    z, y, core = me // 8, (me // 2) % 4, me % 2
    every = range(BLOCKS)
    along_z = [[(i, (i + 8 * d) % 32) for i in every] for d in range(NEAR)]
    along_y = [[(i, i // 8 * 8 + (i + 2 * d) % 8) for i in every] for d in range(NEAR)]

    def filter_for(d):
        part = lax.dynamic_slice_in_dim(filter_taps, (z + d) % NEAR * GROUP, GROUP, 1)
        return lax.ppermute(part, "seq", along_z[d]) if d else part

    turned = pl.pallas_call(
        turn_kernel,
        out_shape=jax.ShapeDtypeStruct((NEAR, NEAR, 2, QUARTERS * PACK, SIDE), BF16),
        compiler_params=small,
        cost_estimate=pl.CostEstimate(flops=2 * 10**10, bytes_accessed=2**20, transcendentals=0),
        name="turn",
    )(*[filter_for(d) for d in TURN_ORDER])

    def turned_for(d):
        part = lax.dynamic_index_in_dim(turned, (y + d) % NEAR, 0, keepdims=False)
        return lax.ppermute(part, "seq", along_y[d]) if d else part

    bands = [turned_for(d) for d in BAND_ORDER]
    hbm = pl.BlockSpec(memory_space=pl.ANY)
    vmem = pl.BlockSpec(memory_space=pltpu.VMEM)
    smem = pl.BlockSpec(memory_space=pltpu.SMEM)
    place = me.astype(jnp.int32)[None]

    def for_other(blocks, ready):
        return pl.pallas_call(
            other_kernel,
            in_specs=[smem] + [vmem] * 4 + [hbm],
            out_shape=jax.ShapeDtypeStruct((NEAR, NEAR, *blocks[0].shape[2:]), BF16),
            compiler_params=small,
            name="other",
        )(place, *blocks, ready)

    to_other = for_other(bands, halo)
    from_other = lax.ppermute(to_other, "seq", [(i, i ^ 1) for i in every])

    product_sent = pl.pallas_call(
        product_kernel,
        in_specs=[vmem, vmem, vmem],
        out_specs=vmem,
        out_shape=jax.ShapeDtypeStruct((BLOCKS, OUT_TILES * PACK, SIDE), BF16),
        scratch_shapes=[
            pltpu.VMEM((TOKENS + 8, CHANS), F32),
            pltpu.VMEM((TOKENS + 8, CHANS), F32),
            pltpu.VMEM((TOKENS, CHANS), F32),
            pltpu.VMEM((SIDE, CHANS), F32),
        ],
        compiler_params=small,
        cost_estimate=pl.CostEstimate(flops=2 * 10**10, bytes_accessed=2**22, transcendentals=0),
        name="product",
    )(key_input, value_input, short_taps)
    product_arrived = swap(product_sent)

    work = pltpu.VMEM((BLOCKS, QUARTERS, PACK, SIDE), F32)
    conv, hops = pl.pallas_call(
        middle_kernel,
        in_specs=[smem] + [vmem] * 8,
        out_shape=[
            jax.ShapeDtypeStruct((BLOCKS, HALF_ROWS + PACK, SIDE), BF16),
            jax.ShapeDtypeStruct((BLOCKS, HALF_ROWS, SIDE), BF16),
        ],
        scratch_shapes=[work, work, work],
        compiler_params=small,
        cost_estimate=pl.CostEstimate(flops=8 * 10**9, bytes_accessed=2 * 10**6, transcendentals=0),
        name="middle",
    )(place, product_arrived, *bands, from_other, *[jnp.asarray(c) for c in consts])

    def conv_for(d):
        part = lax.dynamic_slice_in_dim(hops, (z + d) % NEAR * 8, 8, 0)
        return lax.ppermute(part, "seq", along_z[d]) if d else part

    picked = pl.pallas_call(
        pick_kernel,
        out_shape=jax.ShapeDtypeStruct((NEAR, NEAR, 2, HALF_ROWS, SIDE), BF16),
        compiler_params=small,
        cost_estimate=pl.CostEstimate(flops=2 * 10**10, bytes_accessed=2**20, transcendentals=0),
        name="pick",
    )(*[conv_for(d) for d in range(NEAR)])

    def picked_for(d):
        part = lax.dynamic_index_in_dim(picked, (y + d) % NEAR, 0, keepdims=False)
        return lax.ppermute(part, "seq", along_y[d]) if d else part

    returned = swap(conv)
    conv_bands = [picked_for(d) for d in BAND_ORDER]
    pad = pltpu.VMEM((TOKENS + 8, CHANS), F32)
    query_mix, direct = pl.pallas_call(
        gate_kernel,
        in_specs=[hbm] * 3 + [vmem] * 3 + [hbm],
        out_shape=[jax.ShapeDtypeStruct((TOKENS, CHANS), F32)] * 2,
        scratch_shapes=[pltpu.VMEM((3, TOKENS, CHANS), BF16), pad, pad, pad, pltpu.SemaphoreType.DMA((3,))],
        compiler_params=small,
        cost_estimate=pl.CostEstimate(flops=10**9, bytes_accessed=4 * 10**6, transcendentals=0),
        name="gate",
    )(query_input, key_input, value_input, halo, short_taps, skip_gain[None, :], picked)
    conv_to_other = for_other(conv_bands, direct)
    conv_from_other = lax.ppermute(conv_to_other, "seq", [(i, i ^ 1) for i in every])
    return pl.pallas_call(
        end_kernel,
        in_specs=[smem] + [vmem] * 8,
        out_specs=hbm,
        out_shape=jax.ShapeDtypeStruct((TOKENS, CHANS), BF16),
        scratch_shapes=[
            pltpu.VMEM((BLOCKS, HALF_ROWS, SIDE), BF16),
            pltpu.VMEM((TOKENS, CHANS), BF16),
            pltpu.SemaphoreType.DMA((QUARTERS,)),
        ],
        compiler_params=small,
        name="end",
    )(place, query_mix, direct, returned, *conv_bands, conv_from_other)


def solution(mesh):
    placed = (
        P("seq", "chan"),
        P("seq", "chan"),
        P("seq", "chan"),
        P("seq", "chan"),
        P(None, None, "chan"),
        P("chan"),
    )
    return jax.shard_map(
        functools.partial(local, tables()),
        mesh=mesh,
        in_specs=placed,
        out_specs=P("seq", "chan"),
        check_vma=False,
    )
```
